128 devices in a mesh: tile: 16 (over x, y), chan: 8 (over z, core).
Axes of the slice: x: 4, y: 4, z: 4, core: 2. Of those that a mesh axis runs over, the one named last changes fastest.
Arguments:
- fields: bfloat16 [12, 128, 128, 256], P(None, 'tile', 'chan'), may hold values from -6 to 6
- neighbour: int32 [12, 4], replicated, may hold values from 0 to 11
- rotation: int32 [12, 4], replicated, may hold values from 0 to 3
- conv_weight: float32 [7, 7, 256], replicated, may hold values from -0.875 to 0.875
- conv_bias: float32 [256], replicated, may hold values from -3 to 3
- norm_gain: float32 [256], replicated, may hold values from 0.25 to 1.75
- norm_shift: float32 [256], replicated, may hold values from -3 to 3
- weight_in: bfloat16 [256, 1024], replicated, may hold values from -0.375 to 0.375
- bias_in: float32 [1024], replicated, may hold values from -3 to 3
- weight_out: bfloat16 [1024, 256], replicated, may hold values from -0.1875 to 0.1875
- bias_out: float32 [256], replicated, may hold values from -3 to 3
- layer_scale: float32 [256], replicated, may hold values from 0.3 to 1.5
Outputs:
- updated: bfloat16 [12, 128, 128, 256], P(None, 'tile', 'chan')
The draws below stay inside these ranges and needn't reach their ends.
All inputs are finite; a program needn't handle non-finite values.
Results may differ from the reference program's by a relative error of at most 0.005.
Values may be sent and summed in bfloat16 or wider, within the bound.
A program may use at most 128 MiB of HBM per device.

```python
import math
from functools import partial
import jax
import jax.numpy as jnp
from jax import lax

F = 128
C = 256
HID = 1024


def place_ends(entries, own_key, least, top_value):
    index_at = [jax.random.randint(jax.random.fold_in(own_key, axis), (), 0, length) for axis, length in enumerate(entries.shape)]
    longest = entries.shape.index(max(entries.shape))
    beside = index_at[:longest] + [(index_at[longest] + 1) % entries.shape[longest]] + index_at[longest + 1:]
    return entries.at[tuple(index_at)].set(least).at[tuple(beside)].set(top_value)


def shard_levels(rng, dims, cuts, smallest, top_value):
    def one(dim, blocks):
        heights = jax.random.uniform(jax.random.fold_in(jax.random.fold_in(rng, 6), dim), (blocks,), jnp.float32, smallest / len(cuts), top_value / len(cuts))
        return jnp.repeat(jnp.exp(heights), dims[dim] // blocks).reshape((-1,) + (1,) * (len(dims) - dim - 1))

    gain = one(*cuts[0])
    for cut in cuts[1:]:
        gain = gain * one(*cut)
    return gain


def normal_values(own_key, extent, deviation, reach, split=(), kind=jnp.bfloat16):
    gain = shard_levels(own_key, extent, split, -0.22, 0.18) if split else 1.0
    drawn = jax.random.normal(own_key, extent, jnp.float32) * deviation * gain
    return jnp.minimum(jnp.maximum(drawn, -reach), reach).astype(kind)


def setup_inputs(seed: int = 0) -> dict:
    streams_of = jax.random.split(jax.random.key(seed), 13)
    fields = normal_values(streams_of[0], (12, F, F, C), 1.0, 6.0, ((1, 16), (2, 8)))
    neighbour = place_ends(jax.random.randint(streams_of[1], (12, 4), 0, 12), jax.random.fold_in(streams_of[1], 1), 0, 11).astype(jnp.int32)
    rotation = place_ends(jax.random.randint(streams_of[2], (12, 4), 0, 4), jax.random.fold_in(streams_of[2], 1), 0, 3).astype(jnp.int32)
    conv_weight = normal_values(streams_of[3], (7, 7, C), 49 ** -0.5, 0.875, (), jnp.float32)
    conv_bias = normal_values(streams_of[4], (C,), 0.5, 3.0, (), jnp.float32)
    norm_gain = jnp.clip(1.0 + 0.15 * jax.random.normal(streams_of[5], (C,), jnp.float32), 0.25, 1.75)
    norm_shift = normal_values(streams_of[6], (C,), 0.5, 3.0, (), jnp.float32)
    weight_in = normal_values(streams_of[7], (C, HID), C ** -0.5, 0.375)
    bias_in = normal_values(streams_of[8], (HID,), 0.5, 3.0, (), jnp.float32)
    weight_out = normal_values(streams_of[9], (HID, C), HID ** -0.5, 0.1875)
    bias_out = normal_values(streams_of[10], (C,), 0.5, 3.0, (), jnp.float32)
    layer_scale = jnp.clip(jnp.exp(jax.random.uniform(streams_of[11], (C,), jnp.float32, math.log(0.3), math.log(1.5))), 0.3, 1.5)
    return {"fields": fields, "neighbour": neighbour, "rotation": rotation, "conv_weight": conv_weight, "conv_bias": conv_bias, "norm_gain": norm_gain, "norm_shift": norm_shift, "weight_in": weight_in, "bias_in": bias_in, "weight_out": weight_out, "bias_out": bias_out, "layer_scale": layer_scale}


def turn_face(face_plane, quarter):
    branches = [partial(jnp.rot90, k=count_turns, axes=(0, 1)) for count_turns in range(4)]
    return lax.switch(quarter, branches, face_plane)

def padded_face(fields, neighbour, rotation, face_index):
    centre = fields[face_index]
    upper_rows = turn_face(fields[neighbour[face_index, 0]], rotation[face_index, 0])[-3:]
    left_cols = turn_face(fields[neighbour[face_index, 1]], rotation[face_index, 1])[:, -3:]
    lower_rows = turn_face(fields[neighbour[face_index, 2]], rotation[face_index, 2])[:3]
    right_cols = turn_face(fields[neighbour[face_index, 3]], rotation[face_index, 3])[:, :3]
    middle = jnp.concatenate([upper_rows, centre, lower_rows], axis=0)
    corner = jnp.zeros((3, 3, centre.shape[2]), centre.dtype)
    left_full = jnp.concatenate([corner, left_cols, corner], axis=0)
    right_full = jnp.concatenate([corner, right_cols, corner], axis=0)
    return jnp.concatenate([left_full, middle, right_full], axis=1)

def depthwise(padded, conv_weight, conv_bias):
    height = padded.shape[0] - 6
    breadth = padded.shape[1] - 6
    summed_taps = jnp.zeros((height, breadth, padded.shape[2]), jnp.float32) + conv_bias
    for row_tap in range(7):
        for col_tap in range(7):
            window = padded[row_tap:row_tap + height, col_tap:col_tap + breadth].astype(jnp.float32)
            summed_taps = summed_taps + conv_weight[row_tap, col_tap] * window
    return summed_taps

def block_mlp(rows_in, residual, norm_gain, norm_shift, weight_in, bias_in, weight_out, bias_out, layer_scale):
    values = rows_in.astype(jnp.float32)
    centre_mean = lax.optimization_barrier(jnp.mean(values, axis=-1, keepdims=True))
    spread = lax.optimization_barrier(jnp.mean((values - centre_mean) ** 2, axis=-1, keepdims=True))
    normed = ((values - centre_mean) * lax.rsqrt(spread + 1e-06) * norm_gain + norm_shift).astype(jnp.bfloat16)
    hidden = jax.nn.gelu(jnp.dot(normed, weight_in, preferred_element_type=jnp.float32) + bias_in).astype(jnp.bfloat16)
    update = jnp.dot(hidden, weight_out, preferred_element_type=jnp.float32) + bias_out
    return (residual.astype(jnp.float32) + layer_scale * update).astype(jnp.bfloat16)

def reference(fields, neighbour, rotation, conv_weight, conv_bias, norm_gain, norm_shift, weight_in, bias_in, weight_out, bias_out, layer_scale):
    outputs = []
    for face_index in range(12):
        padded = padded_face(fields, neighbour, rotation, face_index)
        mixed = depthwise(padded, conv_weight, conv_bias).astype(jnp.bfloat16)
        channels = mixed.shape[2]
        result = block_mlp(mixed.reshape(-1, channels), fields[face_index].reshape(-1, channels), norm_gain, norm_shift, weight_in, bias_in, weight_out, bias_out, layer_scale)
        outputs.append(result.reshape(fields[face_index].shape))
    return jnp.stack(outputs)
```

```python
import functools

import jax
import jax.numpy as jnp
from jax import lax
from jax.experimental import pallas as pl
from jax.experimental.pallas import tpu as pltpu
from jax.sharding import PartitionSpec as P

F32, BF16 = jnp.float32, jnp.bfloat16
FACES, ROWS, COLS, CH, HID = 12, 8, 16, 256, 1024
LANES = 128
TILES, CHANS = 16, 8
STRIDE = 32
FIRST = 8
PADROWS = ROWS + 6
SIDES = 4
STRIP = FACES * 8
FACES_AT_ONCE = 4


def relay_of(block, depth):
    n = block * 3 + depth
    return {"tile": 2 + n // 4, "chan": 2 + n % 4}


def each_pair(body):
    lax.fori_loop(0, FACES // 2, lambda pair, c: (body(pair), c)[1], 0)


def each_face(body):
    lax.fori_loop(0, FACES, lambda face, c: (body(face), c)[1], 0)


def lanes(half):
    return pl.ds(half * LANES, LANES)


def pair_rows(pair):
    return pl.ds(pl.multiple_of(pair * 16, 16), 16)


def kernel(
    fields, neighbour, rotation, conv_weight, conv_bias, norm_gain, norm_shift,
    weight_in, bias_in, weight_out, bias_out, layer_scale,
    out,
    x, nbr, rot, cw, cb, gain, shift, w_in, b_in, w_out, b_out, scale,
    taps, padded, acc, result,
    send_left, send_right, send_edge, left, right, top, bottom, seam,
    corner_out_left, corner_out_right, corner_left, corner_right, above, below,
    relay_in, relay_all, relay_out,
    local_sems, send_sems, recv_sems, out_sem,
):
    i, j = lax.axis_index("tile"), lax.axis_index("chan")
    has_up, has_down = i > 0, i < TILES - 1
    has_left, has_right = j > 0, j < CHANS - 1
    is_top, is_bottom = i == 0, i == TILES - 1
    is_left, is_right = j == 0, j == CHANS - 1
    is_relay = (i >= 2) & (i < 14) & (j >= 2) & (j < 6)
    number = (i - 2) * 4 + (j - 2)
    block, depth = number // 3, number % 3
    turned_block = 15 - block

    locals_ = [
        pltpu.make_async_copy(src, dst, local_sems.at[n])
        for n, (src, dst) in enumerate(
            [
                (fields, x), (neighbour, nbr), (rotation, rot), (conv_weight, cw), (conv_bias, cb),
                (norm_gain, gain), (norm_shift, shift), (weight_in, w_in), (bias_in, b_in),
                (weight_out, w_out), (bias_out, b_out), (layer_scale, scale),
            ]
        )
    ]
    for copy in locals_:
        copy.start()

    barrier = pltpu.get_barrier_semaphore()

    def greet(tile, chan):
        pl.semaphore_signal(
            barrier, inc=1, device_id={"tile": tile, "chan": chan},
            device_id_type=pl.DeviceIdType.MESH,
        )

    def greet_relay(block_, depth_):
        there = relay_of(block_, depth_)
        greet(there["tile"], there["chan"])

    pl.when(has_up)(lambda: greet(i - 1, j))
    pl.when(has_down)(lambda: greet(i + 1, j))
    pl.when(has_left)(lambda: greet(i, j - 1))
    pl.when(has_right)(lambda: greet(i, j + 1))

    @pl.when(is_relay)
    def _():
        greet(0, 7 - block // 2)
        greet(block, 0)
        greet(TILES - 1, block // 2)
        greet(turned_block, CHANS - 1)

    @pl.when(is_top)
    def _():
        for half in range(2):
            for k in range(3):
                greet_relay(2 * j + half, k)

    @pl.when(is_bottom)
    def _():
        for half in range(2):
            for k in range(3):
                greet_relay(15 - (2 * j + half), k)

    def greet_side(to_block):
        for k in range(3):
            greet_relay(to_block(i), k)

        @pl.when(has_up)
        def _():
            for k in range(3):
                greet_relay(to_block(i - 1), k)

        @pl.when(has_down)
        def _():
            for k in range(3):
                greet_relay(to_block(i + 1), k)

    pl.when(is_left)(lambda: greet_side(lambda row: 15 - row))
    pl.when(is_right)(lambda: greet_side(lambda row: row))

    def as_int(flag):
        return flag.astype(jnp.int32)

    expected = (
        as_int(has_up) + as_int(has_down) + as_int(has_left) + as_int(has_right)
        + 6 * as_int(is_top) + 6 * as_int(is_bottom) + 3 * as_int(is_left) + 3 * as_int(is_right)
        + as_int(is_relay) * (4 + 2 * (as_int(block > 0) + as_int(block < 15)))
    )

    locals_[0].wait()

    def unpack(face):
        for half in range(2):
            for r in range(ROWS):
                padded[face, half, pl.ds((r + 3) * STRIDE + FIRST, COLS), :] = x[
                    face, r, :, lanes(half)
                ].astype(F32)
        zero = jnp.zeros((8, LANES), F32)
        for half in range(2):
            for r in (0, 1, 2, 11, 12, 13):
                padded[face, half, pl.ds(r * STRIDE, 8), :] = zero
                padded[face, half, pl.ds(r * STRIDE + FIRST + COLS, 8), :] = zero

    each_face(unpack)

    def column(face, half, first_row, c):
        return padded[face, half, pl.ds(first_row * STRIDE + c + FIRST, 8, stride=STRIDE), :]

    def pack_columns(pair):
        for half in range(2):
            for k in range(3):
                for target, c in ((send_left, k), (send_right, COLS - 1 - k)):
                    target[k, pair_rows(pair), lanes(half)] = jnp.concatenate(
                        [column(2 * pair + e, half, 3, c) for e in range(2)], axis=0
                    ).astype(BF16)

    each_pair(pack_columns)

    def pack_edge(row_of):
        def body(pair):
            for half in range(2):
                for seg in range(2):
                    for k in range(3):
                        at = pl.ds((row_of(k) + 3) * STRIDE + FIRST + 8 * seg, 8)
                        send_edge[seg, k, pair_rows(pair), lanes(half)] = jnp.concatenate(
                            [padded[2 * pair + e, half, at, :] for e in range(2)], axis=0
                        ).astype(BF16)

        each_pair(body)

    pl.when(is_top)(lambda: pack_edge(lambda k: k))
    pl.when(is_bottom)(lambda: pack_edge(lambda k: ROWS - 1 - k))

    pl.semaphore_wait(barrier, expected)

    def remote(src, dst, send, recv, where):
        return pltpu.make_async_remote_copy(
            src_ref=src, dst_ref=dst, send_sem=send_sems.at[send], recv_sem=recv_sems.at[recv],
            device_id=where, device_id_type=pl.DeviceIdType.MESH,
        )

    LEFT, RIGHT, TOP, BOTTOM, SEAM, CORNER_L, CORNER_R, ABOVE, BELOW, RELAY = range(10)

    edge_sends = [
        (is_top, [
            remote(send_edge.at[seg, k], relay_in.at[0], 3 * seg + k, RELAY,
                   relay_of(15 - (2 * j + seg), k))
            for seg in range(2) for k in range(3)
        ]),
        (is_bottom, [
            remote(send_edge.at[seg, k], relay_in.at[2], 3 * seg + k, RELAY,
                   relay_of(2 * j + seg, k))
            for seg in range(2) for k in range(3)
        ]),
        (is_left, [
            remote(send_left.at[k], relay_in.at[1], 6 + k, RELAY, relay_of(i, k))
            for k in range(3)
        ]),
        (is_right, [
            remote(send_right.at[k], relay_in.at[3], 6 + k, RELAY, relay_of(15 - i, k))
            for k in range(3)
        ]),
    ]
    halo_sends = [
        (has_up, [remote(x.at[:, pl.ds(0, 3)], bottom, 9, BOTTOM, {"tile": i - 1, "chan": j})]),
        (has_down, [remote(x.at[:, pl.ds(ROWS - 3, 3)], top, 10, TOP, {"tile": i + 1, "chan": j})]),
        (has_left, [remote(send_left, right, 11, RIGHT, {"tile": i, "chan": j - 1})]),
        (has_right, [remote(send_right, left, 12, LEFT, {"tile": i, "chan": j + 1})]),
    ]
    corner_sends = [
        (has_left, [remote(corner_out_left, corner_right, 13, CORNER_R, {"tile": i, "chan": j - 1})]),
        (has_right, [remote(corner_out_right, corner_left, 14, CORNER_L, {"tile": i, "chan": j + 1})]),
    ]
    relay_sends = [
        (is_relay, [
            remote(relay_out.at[0], seam.at[block % 2, depth], 15, SEAM,
                   {"tile": 0, "chan": block // 2}),
            remote(relay_out.at[2], seam.at[turned_block % 2, depth], 16, SEAM,
                   {"tile": TILES - 1, "chan": turned_block // 2}),
            remote(relay_out.at[1], left.at[depth], 17, LEFT, {"tile": turned_block, "chan": 0}),
            remote(relay_out.at[3], right.at[depth], 18, RIGHT, {"tile": block, "chan": CHANS - 1}),
        ]),
        (is_relay & (turned_block < 15), [
            remote(relay_out.at[1], above.at[depth], 19, ABOVE, {"tile": turned_block + 1, "chan": 0}),
        ]),
        (is_relay & (turned_block > 0), [
            remote(relay_out.at[1], below.at[depth], 20, BELOW, {"tile": turned_block - 1, "chan": 0}),
        ]),
        (is_relay & (block < 15), [
            remote(relay_out.at[3], above.at[depth], 21, ABOVE, {"tile": block + 1, "chan": CHANS - 1}),
        ]),
        (is_relay & (block > 0), [
            remote(relay_out.at[3], below.at[depth], 22, BELOW, {"tile": block - 1, "chan": CHANS - 1}),
        ]),
    ]

    def start_all(sends):
        for condition, copies in sends:
            @pl.when(condition)
            def _():
                for copy in copies:
                    copy.start()

    def arrived(buffer, recv):
        pltpu.make_async_copy(buffer, buffer, recv_sems.at[recv]).wait()

    start_all(edge_sends)
    start_all(halo_sends)

    locals_[1].wait()
    locals_[2].wait()

    @pl.when(is_relay)
    def _():
        arrived(relay_in, RELAY)
        row = lax.broadcasted_iota(jnp.int32, (STRIP, STRIP), 0)
        col = lax.broadcasted_iota(jnp.int32, (STRIP, STRIP), 1)
        turn = (row // 8 * 8 + 7 - row % 8 == col).astype(BF16)
        for side in range(SIDES):
            strip = relay_in[side]
            relay_all[0, pl.ds(side * FACES, FACES)] = strip.astype(F32).reshape(FACES, 8, CH)
            relay_all[1, pl.ds(side * FACES, FACES)] = jnp.dot(
                turn, strip, preferred_element_type=F32
            ).reshape(FACES, 8, CH)

        def choose(pair):
            for side in range(SIDES):
                chosen = []
                for e in range(2):
                    source = (side + 6 - rot[2 * pair + e, side]) & 3
                    same = ((source + 1) & 3) >> 1
                    flip = same if side in (1, 2) else 1 - same
                    chosen.append(relay_all[flip, source * FACES + nbr[2 * pair + e, side]])
                relay_out[side, pair_rows(pair), :] = jnp.concatenate(chosen, axis=0).astype(BF16)

        each_pair(choose)

    start_all(relay_sends)

    locals_[3].wait()
    locals_[4].wait()
    for half in range(2):
        for a in range(7):
            for b in range(7):
                taps[half, a * 7 + b] = jnp.broadcast_to(cw[a, pl.ds(b, 1), lanes(half)], (8, LANES))

    def convolve(face, half, group, total, rows, shifts):
        for b in shifts:
            cells = {
                r: padded[face, half, pl.ds(r * STRIDE + FIRST - 3 + b + 8 * group, 8), :]
                for r in rows
            }
            for a in range(7):
                tap = taps[half, a * 7 + b]
                for r in range(ROWS):
                    if r + a in cells and r in total:
                        total[r] = total[r] + tap * cells[r + a]
        return total

    own = range(3, 11)
    groups = [(half, group) for half in range(2) for group in range(2)]

    def total_of(face, half, group, rows):
        return {r: acc[face, r, pl.ds(8 * group, 8), lanes(half)] for r in rows}

    def keep(face, half, group, total):
        for r, value in total.items():
            acc[face, r, pl.ds(8 * group, 8), lanes(half)] = value

    def inner(face):
        for half, group in groups:
            bias = jnp.broadcast_to(cb[:, lanes(half)], (8, LANES))
            total = {r: bias for r in range(ROWS)}
            shifts = range(3, 7) if group == 0 else range(4)
            keep(face, half, group, convolve(face, half, group, total, own, shifts))

    each_face(inner)

    def unpack_rows(buffer, first_row):
        def body(face):
            for half in range(2):
                for r in range(3):
                    padded[face, half, pl.ds((first_row + r) * STRIDE + FIRST, COLS), :] = buffer[
                        face, r, :, lanes(half)
                    ].astype(F32)

        each_face(body)

    def unpack_seam(row_of):
        def body(pair):
            for half in range(2):
                for seg in range(2):
                    for k in range(3):
                        both = seam[seg, k, pair_rows(pair), lanes(half)].astype(F32)
                        for e in range(2):
                            padded[
                                2 * pair + e, half, pl.ds(row_of(k) * STRIDE + FIRST + 8 * seg, 8), :
                            ] = both[8 * e : 8 * e + 8]

        each_pair(body)

    @pl.when(has_up)
    def _():
        arrived(top, TOP)
        unpack_rows(top, 0)

    @pl.when(has_down)
    def _():
        arrived(bottom, BOTTOM)
        unpack_rows(bottom, 11)

    @pl.when(is_top)
    def _():
        arrived(seam, SEAM)
        unpack_seam(lambda k: 2 - k)

    @pl.when(is_bottom)
    def _():
        arrived(seam, SEAM)
        unpack_seam(lambda k: 11 + k)

    sublane = lax.broadcasted_iota(jnp.int32, (8, LANES), 0)

    def pack_corners(pair):
        for half in range(2):
            for k in range(3):
                for target, c in ((corner_out_left, k), (corner_out_right, COLS - 1 - k)):
                    target[k, pair_rows(pair), lanes(half)] = jnp.concatenate(
                        [
                            jnp.where(
                                sublane < 4,
                                column(2 * pair + e, half, 0, c),
                                column(2 * pair + e, half, 6, c),
                            )
                            for e in range(2)
                        ],
                        axis=0,
                    ).astype(BF16)

    each_pair(pack_corners)
    start_all(corner_sends)

    def unpack_columns(buffer, col_of):
        def body(pair):
            for half in range(2):
                for k in range(3):
                    both = buffer[k, pair_rows(pair), lanes(half)].astype(F32)
                    for e in range(2):
                        padded[
                            2 * pair + e, half,
                            pl.ds(3 * STRIDE + FIRST + col_of(k), 8, stride=STRIDE), :
                        ] = both[8 * e : 8 * e + 8]

        each_pair(body)

    def unpack_corner(buffer, col_of, parts):
        def body(pair):
            for half in range(2):
                for k in range(3):
                    both = buffer[k, pair_rows(pair), lanes(half)].astype(F32)
                    for e in range(2):
                        for sub, row in parts:
                            padded[
                                2 * pair + e, half,
                                pl.ds(row * STRIDE + FIRST + col_of(k), 3, stride=STRIDE), :
                            ] = both[8 * e + sub : 8 * e + sub + 3]

        each_pair(body)

    def at_left(k):
        return -1 - k

    def at_right(k):
        return COLS + k

    arrived(left, LEFT)
    unpack_columns(left, at_left)
    arrived(right, RIGHT)
    unpack_columns(right, at_right)

    def sides(face):
        for half, group in groups:
            total = total_of(face, half, group, range(ROWS))
            shifts = range(3) if group == 0 else range(4, 7)
            keep(face, half, group, convolve(face, half, group, total, own, shifts))

    each_face(sides)

    @pl.when(has_left)
    def _():
        arrived(corner_left, CORNER_L)
        unpack_corner(corner_left, at_left, ((0, 0), (5, 11)))

    @pl.when(has_right)
    def _():
        arrived(corner_right, CORNER_R)
        unpack_corner(corner_right, at_right, ((0, 0), (5, 11)))

    for at_edge, col_of in ((is_left, at_left), (is_right, at_right)):
        @pl.when(at_edge & has_up)
        def _():
            arrived(above, ABOVE)
            unpack_corner(above, col_of, ((5, 0),))

        @pl.when(at_edge & has_down)
        def _():
            arrived(below, BELOW)
            unpack_corner(below, col_of, ((0, 11),))

    def ends(face):
        for half, group in groups:
            for rows, halo in ((range(3), range(3)), (range(5, 8), range(11, 14))):
                total = total_of(face, half, group, rows)
                keep(face, half, group, convolve(face, half, group, total, halo, range(7)))

    each_face(ends)

    for copy in locals_[5:]:
        copy.wait()

    def finished(first):
        return pltpu.make_async_copy(
            result.at[pl.ds(first, FACES_AT_ONCE)], out.at[pl.ds(first, FACES_AT_ONCE)], out_sem
        )

    def pointwise(step, carry):
        first = step * FACES_AT_ONCE
        faces = pl.ds(first, FACES_AT_ONCE)
        cells = FACES_AT_ONCE * ROWS * COLS
        values = acc[faces].reshape(cells, CH).astype(BF16).astype(F32)
        mean = jnp.mean(values, axis=-1, keepdims=True)
        apart = values - mean
        spread = jnp.mean(apart * apart, axis=-1, keepdims=True)
        normed = (apart * lax.rsqrt(spread + 1e-6) * gain[...] + shift[...]).astype(BF16)
        hidden = jnp.dot(normed, w_in[...], preferred_element_type=F32) + b_in[...]
        inner_ = hidden * (0.7978845608028654 + 0.035677408136300125 * (hidden * hidden))
        hidden = (hidden * (1.0 + jnp.tanh(inner_))).astype(BF16)
        update = 0.5 * jnp.dot(hidden, w_out[...], preferred_element_type=F32) + b_out[...]
        residual = x[faces].reshape(cells, CH).astype(F32)
        result[faces] = (residual + scale[...] * update).astype(BF16).reshape(
            FACES_AT_ONCE, ROWS, COLS, CH
        )
        finished(first).start()
        return carry

    lax.fori_loop(0, FACES // FACES_AT_ONCE, pointwise, 0)
    pltpu.make_async_copy(result, out, out_sem).wait()

    for condition, copies in edge_sends + halo_sends + corner_sends + relay_sends:
        @pl.when(condition)
        def _():
            for copy in copies:
                copy.wait_send()


def block(fields, neighbour, rotation, conv_weight, conv_bias, norm_gain, norm_shift,
          weight_in, bias_in, weight_out, bias_out, layer_scale):
    def row(vector):
        return vector.reshape(1, -1)

    anywhere = pl.BlockSpec(memory_space=pl.ANY)
    strip = pltpu.VMEM((3, STRIP, CH), BF16)
    halo_rows = pltpu.VMEM((FACES, 3, COLS, CH), BF16)
    return pl.pallas_call(
        kernel,
        out_shape=jax.ShapeDtypeStruct(fields.shape, BF16),
        in_specs=[anywhere] * 12,
        out_specs=anywhere,
        scratch_shapes=[
            pltpu.VMEM(fields.shape, BF16),
            pltpu.SMEM((FACES, SIDES), jnp.int32),
            pltpu.SMEM((FACES, SIDES), jnp.int32),
            pltpu.VMEM((7, 7, CH), F32),
            pltpu.VMEM((1, CH), F32),
            pltpu.VMEM((1, CH), F32),
            pltpu.VMEM((1, CH), F32),
            pltpu.VMEM((CH, HID), BF16),
            pltpu.VMEM((1, HID), F32),
            pltpu.VMEM((HID, CH), BF16),
            pltpu.VMEM((1, CH), F32),
            pltpu.VMEM((1, CH), F32),
            pltpu.VMEM((2, 49, 8, LANES), F32),
            pltpu.VMEM((FACES, 2, PADROWS * STRIDE, LANES), F32),
            pltpu.VMEM(fields.shape, F32),
            pltpu.VMEM(fields.shape, BF16),
            strip, strip,
            pltpu.VMEM((2, 3, STRIP, CH), BF16),
            strip, strip,
            halo_rows, halo_rows,
            pltpu.VMEM((2, 3, STRIP, CH), BF16),
            strip, strip, strip, strip, strip, strip,
            pltpu.VMEM((SIDES, STRIP, CH), BF16),
            pltpu.VMEM((2, SIDES * FACES, 8, CH), F32),
            pltpu.VMEM((SIDES, STRIP, CH), BF16),
            pltpu.SemaphoreType.DMA((12,)),
            pltpu.SemaphoreType.DMA((23,)),
            pltpu.SemaphoreType.DMA((10,)),
            pltpu.SemaphoreType.DMA,
        ],
        compiler_params=pltpu.CompilerParams(
            collective_id=0, has_side_effects=True, vmem_limit_bytes=48 * 2**20
        ),
        name="convnext_block",
    )(
        fields, neighbour, rotation, conv_weight, row(conv_bias), row(norm_gain), row(norm_shift),
        weight_in, row(bias_in), weight_out, row(bias_out), row(layer_scale),
    )


def solution(mesh):
    cells = P(None, "tile", "chan", None)
    return jax.shard_map(
        block, mesh=mesh, in_specs=(cells,) + (P(),) * 11, out_specs=cells, check_vma=False
    )
```

```python
import functools

import jax
import jax.numpy as jnp
from jax import lax
from jax.experimental import pallas as pl
from jax.experimental.pallas import tpu as pltpu
from jax.sharding import PartitionSpec as P

F32, BF16 = jnp.float32, jnp.bfloat16
FACES, ROWS, COLS, CH, HID = 12, 8, 16, 256, 1024
LANES = 128
TILES, CHANS = 16, 8
STRIDE = 32
FIRST = 8
PADROWS = ROWS + 6
SIDES = 4
STRIP = FACES * 8
FACES_AT_ONCE = 4


def relay_chan(z):
    return z + 1 + 2 * (z // 2)


def relay_of(block, half):
    x, y = block // 4, block % 4
    if half == 0:
        across, along, z = 3 - y, (5 - x) % 4, (y + 1) % 4
    else:
        across, along, z = y, (x + 2) % 4, (6 - y) % 4
    return {"tile": 4 * across + along, "chan": relay_chan(z)}


def relay_role(i, j):
    across, along = i // 4, i % 4
    first = j == relay_chan((4 - across) % 4)
    second = j == relay_chan((6 - across) % 4)
    block = jnp.where(
        second, 4 * ((along + 2) % 4) + across, 4 * ((5 - along) % 4) + 3 - across
    )
    return first | second, block, second.astype(jnp.int32)


def each_quad(body):
    lax.fori_loop(0, FACES // 4, lambda quad, c: (body(quad), c)[1], 0)


def each_pair(body):
    lax.fori_loop(0, FACES // 2, lambda pair, c: (body(pair), c)[1], 0)


def each_face(body):
    lax.fori_loop(0, FACES, lambda face, c: (body(face), c)[1], 0)


def lanes(half):
    return pl.ds(half * LANES, LANES)


def pair_rows(pair):
    return pl.ds(pl.multiple_of(pair * 16, 16), 16)


def kernel(
    fields, neighbour, rotation, conv_weight, conv_bias, norm_gain, norm_shift,
    weight_in, bias_in, weight_out, bias_out, layer_scale,
    out,
    x, nbr, rot, cw, cb, gain, shift, w_in, b_in, w_out, b_out, scale,
    taps, padded, acc, result,
    send_left, send_right, send_edge, send_corner, left, right, top, bottom, seam, corner,
    relay_in, relay_all, relay_out, relay_first, relay_last,
    local_sems, send_sems, recv_sems, out_sem,
):
    i, j = lax.axis_index("tile"), lax.axis_index("chan")
    has_up, has_down = i > 0, i < TILES - 1
    has_left, has_right = j > 0, j < CHANS - 1
    is_top, is_bottom = i == 0, i == TILES - 1
    is_left, is_right = j == 0, j == CHANS - 1
    is_relay, block, my_half = relay_role(i, j)
    turned_block = 15 - block
    odd = block % 2 == 1

    locals_ = [
        pltpu.make_async_copy(src, dst, local_sems.at[n])
        for n, (src, dst) in enumerate(
            [
                (fields, x), (neighbour, nbr), (rotation, rot), (conv_weight, cw), (conv_bias, cb),
                (norm_gain, gain), (norm_shift, shift), (weight_in, w_in), (bias_in, b_in),
                (weight_out, w_out), (bias_out, b_out), (layer_scale, scale),
            ]
        )
    ]
    for copy in locals_:
        copy.start()

    barrier = pltpu.get_barrier_semaphore()

    def greet(tile, chan):
        pl.semaphore_signal(
            barrier, inc=1, device_id={"tile": tile, "chan": chan},
            device_id_type=pl.DeviceIdType.MESH,
        )

    def greet_relays(block_):
        for half in range(2):
            there = relay_of(block_, half)
            greet(there["tile"], there["chan"])

    pl.when(has_up)(lambda: greet(i - 1, j))
    pl.when(has_down)(lambda: greet(i + 1, j))
    pl.when(has_left)(lambda: greet(i, j - 1))
    pl.when(has_right)(lambda: greet(i, j + 1))
    pl.when(has_up & has_left)(lambda: greet(i - 1, j - 1))
    pl.when(has_up & has_right)(lambda: greet(i - 1, j + 1))
    pl.when(has_down & has_left)(lambda: greet(i + 1, j - 1))
    pl.when(has_down & has_right)(lambda: greet(i + 1, j + 1))

    @pl.when(is_relay)
    def _():
        greet(0, 7 - block // 2)
        greet(block, 0)
        greet(TILES - 1, block // 2)
        greet(turned_block, CHANS - 1)

    def greet_end(to_block):
        greet_relays(to_block(2 * j))
        greet_relays(to_block(2 * j + 1))
        pl.when(has_left)(lambda: greet_relays(to_block(2 * j - 1)))
        pl.when(has_right)(lambda: greet_relays(to_block(2 * j + 2)))

    def greet_side(to_block):
        greet_relays(to_block(i))
        pl.when(has_up)(lambda: greet_relays(to_block(i - 1)))
        pl.when(has_down)(lambda: greet_relays(to_block(i + 1)))

    pl.when(is_top)(lambda: greet_end(lambda t: t))
    pl.when(is_bottom)(lambda: greet_end(lambda t: 15 - t))
    pl.when(is_left)(lambda: greet_side(lambda t: 15 - t))
    pl.when(is_right)(lambda: greet_side(lambda t: t))

    def as_int(flag):
        return flag.astype(jnp.int32)

    not_first, not_last = as_int(block > 0), as_int(block < 15)
    expected = (
        (1 + as_int(has_up) + as_int(has_down)) * (1 + as_int(has_left) + as_int(has_right)) - 1
        + 4 * as_int(is_top) + 4 * as_int(is_bottom) + 2 * as_int(is_left) + 2 * as_int(is_right)
        + as_int(is_relay)
        * (4 + 2 * (not_first + not_last) + 2 * jnp.where(odd, not_last, not_first))
    )

    locals_[0].wait()

    def unpack(face):
        for half in range(2):
            for r in range(ROWS):
                padded[face, half, pl.ds((r + 3) * STRIDE + FIRST, COLS), :] = x[
                    face, r, :, lanes(half)
                ].astype(F32)
        zero = jnp.zeros((8, LANES), F32)
        for half in range(2):
            for r in (0, 1, 2, 11, 12, 13):
                padded[face, half, pl.ds(r * STRIDE, 8), :] = zero
                padded[face, half, pl.ds(r * STRIDE + FIRST + COLS, 8), :] = zero

    each_face(unpack)

    def column(face, half, first_row, c):
        return padded[face, half, pl.ds(first_row * STRIDE + c + FIRST, 8, stride=STRIDE), :]

    sublane = lax.broadcasted_iota(jnp.int32, (8, LANES), 0)

    def lower_half(a, b):
        return jnp.where(sublane < 4, a, pltpu.roll(b, 4, 0))

    def upper_half(a, b):
        return jnp.where(sublane < 4, pltpu.roll(a, 4, 0), b)

    def two(a, b):
        return jnp.concatenate([a, b], axis=0).astype(BF16)

    def pack_columns(quad):
        for half in range(2):
            for k in range(3):
                for side, (target, c) in enumerate(((send_left, k), (send_right, COLS - 1 - k))):
                    cells = [column(4 * quad + e, half, 3, c) for e in range(4)]
                    for e in range(2):
                        target[half, k, pair_rows(2 * quad + e), :] = two(*cells[2 * e : 2 * e + 2])
                    send_corner[2 * side, half, k, pair_rows(quad), :] = two(
                        lower_half(*cells[:2]), lower_half(*cells[2:])
                    )
                    send_corner[2 * side + 1, half, k, pair_rows(quad), :] = two(
                        upper_half(*cells[:2]), upper_half(*cells[2:])
                    )

    each_quad(pack_columns)

    def pack_edge(row_of):
        def body(pair):
            for half in range(2):
                for seg in range(2):
                    for k in range(3):
                        at = pl.ds((row_of(k) + 3) * STRIDE + FIRST + 8 * seg, 8)
                        send_edge[seg, half, k, pair_rows(pair), :] = two(
                            *[padded[2 * pair + e, half, at, :] for e in range(2)]
                        )

        each_pair(body)

    pl.when(is_top)(lambda: pack_edge(lambda k: k))
    pl.when(is_bottom)(lambda: pack_edge(lambda k: ROWS - 1 - k))

    pl.semaphore_wait(barrier, expected)

    def remote(src, dst, send, recv, where):
        return pltpu.make_async_remote_copy(
            src_ref=src, dst_ref=dst, send_sem=send_sems.at[send], recv_sem=recv_sems.at[recv],
            device_id=where, device_id_type=pl.DeviceIdType.MESH,
        )

    LEFT, RIGHT, TOP, BOTTOM, SEAM, RELAY, CORNER = range(7)

    edge_sends = [
        (is_top, [
            remote(send_edge.at[seg, half], relay_in.at[0], 2 * seg + half, RELAY,
                   relay_of(15 - (2 * j + seg), half))
            for seg in range(2) for half in range(2)
        ]),
        (is_bottom, [
            remote(send_edge.at[seg, half], relay_in.at[2], 2 * seg + half, RELAY,
                   relay_of(2 * j + seg, half))
            for seg in range(2) for half in range(2)
        ]),
        (is_left, [
            remote(send_left.at[half], relay_in.at[1], 4 + half, RELAY, relay_of(i, half))
            for half in range(2)
        ]),
        (is_right, [
            remote(send_right.at[half], relay_in.at[3], 4 + half, RELAY, relay_of(15 - i, half))
            for half in range(2)
        ]),
    ]
    halo_sends = [
        (has_up, [remote(x.at[:, pl.ds(0, 3)], bottom, 6, BOTTOM, {"tile": i - 1, "chan": j})]),
        (has_down, [remote(x.at[:, pl.ds(ROWS - 3, 3)], top, 7, TOP, {"tile": i + 1, "chan": j})]),
        (has_left, [remote(send_left, right, 8, RIGHT, {"tile": i, "chan": j - 1})]),
        (has_right, [remote(send_right, left, 9, LEFT, {"tile": i, "chan": j + 1})]),
    ]
    for side, (there, has_side) in enumerate(((j - 1, has_left), (j + 1, has_right))):
        for end, (tile, has_end) in enumerate(((i - 1, has_up), (i + 1, has_down))):
            mine, theirs = 2 * side + end, 3 - (2 * side + end)
            halo_sends.append((
                has_side & has_end,
                [remote(send_corner.at[mine], corner.at[theirs], 10 + mine, CORNER + theirs,
                        {"tile": tile, "chan": there})],
            ))

    def pass_on(source, corner_at, send, tile, chan):
        return remote(source, corner.at[corner_at, my_half], send, CORNER + corner_at,
                      {"tile": tile, "chan": chan})

    relay_sends = [
        (is_relay, [
            remote(relay_out.at[0], seam.at[block % 2, my_half], 14, SEAM,
                   {"tile": 0, "chan": block // 2}),
            remote(relay_out.at[2], seam.at[turned_block % 2, my_half], 15, SEAM,
                   {"tile": TILES - 1, "chan": turned_block // 2}),
            remote(relay_out.at[1], left.at[my_half], 16, LEFT, {"tile": turned_block, "chan": 0}),
            remote(relay_out.at[3], right.at[my_half], 17, RIGHT,
                   {"tile": block, "chan": CHANS - 1}),
        ]),
        (is_relay & (turned_block < 15),
         [pass_on(relay_last.at[1], 0, 18, turned_block + 1, 0)]),
        (is_relay & (turned_block > 0),
         [pass_on(relay_first.at[1], 1, 19, turned_block - 1, 0)]),
        (is_relay & (block < 15),
         [pass_on(relay_last.at[3], 2, 20, block + 1, CHANS - 1)]),
        (is_relay & (block > 0),
         [pass_on(relay_first.at[3], 3, 21, block - 1, CHANS - 1)]),
        (is_relay & odd & (block < 15), [
            pass_on(relay_last.at[0], 0, 22, 0, block // 2 + 1),
            pass_on(relay_first.at[2], 3, 23, TILES - 1, turned_block // 2 - 1),
        ]),
        (is_relay & ~odd & (block > 0), [
            pass_on(relay_first.at[0], 2, 22, 0, block // 2 - 1),
            pass_on(relay_last.at[2], 1, 23, TILES - 1, turned_block // 2 + 1),
        ]),
    ]

    def start_all(sends):
        for condition, copies in sends:
            @pl.when(condition)
            def _():
                for copy in copies:
                    copy.start()

    def arrived(buffer, recv):
        pltpu.make_async_copy(buffer, buffer, recv_sems.at[recv]).wait()

    start_all(edge_sends)
    start_all(halo_sends)

    locals_[1].wait()
    locals_[2].wait()

    @pl.when(is_relay)
    def _():
        arrived(relay_in, RELAY)
        row = lax.broadcasted_iota(jnp.int32, (STRIP, STRIP), 0)
        col = lax.broadcasted_iota(jnp.int32, (STRIP, STRIP), 1)
        turn = (row // 8 * 8 + 7 - row % 8 == col).astype(BF16)
        for side in range(SIDES):
            for k in range(3):
                strip = relay_in[side, k]
                at = pl.ds(side * FACES, FACES)
                relay_all[0, at, k] = strip.astype(F32).reshape(FACES, 8, LANES)
                relay_all[1, at, k] = jnp.dot(turn, strip, preferred_element_type=F32).reshape(
                    FACES, 8, LANES
                )

        def choose(quad):
            for side in range(SIDES):
                chosen = []
                for e in range(4):
                    source = (side + 6 - rot[side, 4 * quad + e]) & 3
                    same = ((source + 1) & 3) >> 1
                    flip = same if side in (1, 2) else 1 - same
                    chosen.append(relay_all[flip, source * FACES + nbr[side, 4 * quad + e]])
                for k in range(3):
                    cells = [strip[k] for strip in chosen]
                    for e in range(2):
                        relay_out[side, k, pair_rows(2 * quad + e), :] = two(
                            *cells[2 * e : 2 * e + 2]
                        )
                    relay_first[side, k, pair_rows(quad), :] = two(
                        lower_half(*cells[:2]), lower_half(*cells[2:])
                    )
                    relay_last[side, k, pair_rows(quad), :] = two(
                        upper_half(*cells[:2]), upper_half(*cells[2:])
                    )

        each_quad(choose)

    start_all(relay_sends)

    locals_[3].wait()
    locals_[4].wait()
    for half in range(2):
        for a in range(7):
            for b in range(7):
                taps[half, a * 7 + b] = jnp.broadcast_to(cw[a, pl.ds(b, 1), lanes(half)], (8, LANES))

    def convolve(face, half, group, total, rows, shifts):
        for b in shifts:
            cells = {
                r: padded[face, half, pl.ds(r * STRIDE + FIRST - 3 + b + 8 * group, 8), :]
                for r in rows
            }
            for a in range(7):
                tap = taps[half, a * 7 + b]
                for r in range(ROWS):
                    if r + a in cells and r in total:
                        total[r] = total[r] + tap * cells[r + a]
        return total

    own = range(3, 11)
    groups = [(half, group) for half in range(2) for group in range(2)]

    def total_of(face, half, group, rows):
        return {r: acc[face, r, pl.ds(8 * group, 8), lanes(half)] for r in rows}

    def keep(face, half, group, total):
        for r, value in total.items():
            acc[face, r, pl.ds(8 * group, 8), lanes(half)] = value

    def inner(face):
        for half, group in groups:
            bias = jnp.broadcast_to(cb[:, lanes(half)], (8, LANES))
            total = {r: bias for r in range(ROWS)}
            shifts = range(3, 7) if group == 0 else range(4)
            keep(face, half, group, convolve(face, half, group, total, own, shifts))

    each_face(inner)

    def unpack_rows(buffer, first_row):
        def body(face):
            for half in range(2):
                for r in range(3):
                    padded[face, half, pl.ds((first_row + r) * STRIDE + FIRST, COLS), :] = buffer[
                        face, r, :, lanes(half)
                    ].astype(F32)

        each_face(body)

    def unpack_seam(row_of):
        def body(pair):
            for half in range(2):
                for seg in range(2):
                    for k in range(3):
                        both = seam[seg, half, k, pair_rows(pair), :].astype(F32)
                        for e in range(2):
                            padded[
                                2 * pair + e, half, pl.ds(row_of(k) * STRIDE + FIRST + 8 * seg, 8), :
                            ] = both[8 * e : 8 * e + 8]

        each_pair(body)

    @pl.when(has_up)
    def _():
        arrived(top, TOP)
        unpack_rows(top, 0)

    @pl.when(has_down)
    def _():
        arrived(bottom, BOTTOM)
        unpack_rows(bottom, 11)

    @pl.when(is_top)
    def _():
        arrived(seam, SEAM)
        unpack_seam(lambda k: 2 - k)

    @pl.when(is_bottom)
    def _():
        arrived(seam, SEAM)
        unpack_seam(lambda k: 11 + k)

    def unpack_columns(buffer, col_of):
        def body(pair):
            for half in range(2):
                for k in range(3):
                    both = buffer[half, k, pair_rows(pair), :].astype(F32)
                    for e in range(2):
                        padded[
                            2 * pair + e, half,
                            pl.ds(3 * STRIDE + FIRST + col_of(k), 8, stride=STRIDE), :
                        ] = both[8 * e : 8 * e + 8]

        each_pair(body)

    def unpack_corner(at, beside, end):
        first_col = -4 if at < 2 else COLS

        def body(quad):
            for half in range(2):
                for k in range(3):
                    cells = corner[at, half, k, pair_rows(quad), :].astype(F32)
                    for e in range(4):
                        if beside:
                            col = -1 - k if at < 2 else COLS + k
                            first, row = (1, 0) if end == 0 else (0, 11)
                            padded[
                                4 * quad + e, half,
                                pl.ds(row * STRIDE + FIRST + col, 3, stride=STRIDE), :
                            ] = cells[4 * e + first : 4 * e + first + 3]
                        else:
                            row = 2 - k if end == 0 else 11 + k
                            padded[
                                4 * quad + e, half, pl.ds(row * STRIDE + FIRST + first_col, 4), :
                            ] = cells[4 * e : 4 * e + 4]

        each_quad(body)

    def at_left(k):
        return -1 - k

    def at_right(k):
        return COLS + k

    arrived(left, LEFT)
    unpack_columns(left, at_left)
    arrived(right, RIGHT)
    unpack_columns(right, at_right)

    def sides(face):
        for half, group in groups:
            total = total_of(face, half, group, range(ROWS))
            shifts = range(3) if group == 0 else range(4, 7)
            keep(face, half, group, convolve(face, half, group, total, own, shifts))

    each_face(sides)

    for side, (has_side, at_side) in enumerate(((has_left, is_left), (has_right, is_right))):
        for end, (has_end, at_end) in enumerate(((has_up, is_top), (has_down, is_bottom))):
            at = 2 * side + end

            @pl.when(has_side | has_end)
            def _():
                arrived(corner.at[at], CORNER + at)

            pl.when(has_end)(functools.partial(unpack_corner, at, True, end))
            pl.when(at_end & has_side)(functools.partial(unpack_corner, at, False, end))

    def ends(face):
        for half, group in groups:
            for rows, halo in ((range(3), range(3)), (range(5, 8), range(11, 14))):
                total = total_of(face, half, group, rows)
                keep(face, half, group, convolve(face, half, group, total, halo, range(7)))

    each_face(ends)

    for copy in locals_[5:]:
        copy.wait()

    def finished(first):
        return pltpu.make_async_copy(
            result.at[pl.ds(first, FACES_AT_ONCE)], out.at[pl.ds(first, FACES_AT_ONCE)], out_sem
        )

    def pointwise(step, carry):
        first = step * FACES_AT_ONCE
        faces = pl.ds(first, FACES_AT_ONCE)
        cells = FACES_AT_ONCE * ROWS * COLS
        values = acc[faces].reshape(cells, CH).astype(BF16).astype(F32)
        mean = jnp.mean(values, axis=-1, keepdims=True)
        apart = values - mean
        spread = jnp.mean(apart * apart, axis=-1, keepdims=True)
        normed = (apart * lax.rsqrt(spread + 1e-6) * gain[...] + shift[...]).astype(BF16)
        hidden = jnp.dot(normed, w_in[...], preferred_element_type=F32) + b_in[...]
        inner_ = hidden * (0.7978845608028654 + 0.035677408136300125 * (hidden * hidden))
        hidden = (hidden * (1.0 + jnp.tanh(inner_))).astype(BF16)
        update = 0.5 * jnp.dot(hidden, w_out[...], preferred_element_type=F32) + b_out[...]
        residual = x[faces].reshape(cells, CH).astype(F32)
        result[faces] = (residual + scale[...] * update).astype(BF16).reshape(
            FACES_AT_ONCE, ROWS, COLS, CH
        )
        finished(first).start()
        return carry

    lax.fori_loop(0, FACES // FACES_AT_ONCE, pointwise, 0)
    pltpu.make_async_copy(result, out, out_sem).wait()

    for condition, copies in edge_sends + halo_sends + relay_sends:
        @pl.when(condition)
        def _():
            for copy in copies:
                copy.wait_send()


def block(fields, neighbour, rotation, conv_weight, conv_bias, norm_gain, norm_shift,
          weight_in, bias_in, weight_out, bias_out, layer_scale):
    def row(vector):
        return vector.reshape(1, -1)

    anywhere = pl.BlockSpec(memory_space=pl.ANY)
    strip = pltpu.VMEM((2, 3, STRIP, LANES), BF16)
    corners = pltpu.VMEM((4, 2, 3, STRIP // 2, LANES), BF16)
    relayed = pltpu.VMEM((SIDES, 3, STRIP, LANES), BF16)
    relayed_half = pltpu.VMEM((SIDES, 3, STRIP // 2, LANES), BF16)
    halo_rows = pltpu.VMEM((FACES, 3, COLS, CH), BF16)
    return pl.pallas_call(
        kernel,
        out_shape=jax.ShapeDtypeStruct(fields.shape, BF16),
        in_specs=[anywhere] * 12,
        out_specs=anywhere,
        scratch_shapes=[
            pltpu.VMEM(fields.shape, BF16),
            pltpu.SMEM((SIDES, FACES), jnp.int32),
            pltpu.SMEM((SIDES, FACES), jnp.int32),
            pltpu.VMEM((7, 7, CH), F32),
            pltpu.VMEM((1, CH), F32),
            pltpu.VMEM((1, CH), F32),
            pltpu.VMEM((1, CH), F32),
            pltpu.VMEM((CH, HID), BF16),
            pltpu.VMEM((1, HID), F32),
            pltpu.VMEM((HID, CH), BF16),
            pltpu.VMEM((1, CH), F32),
            pltpu.VMEM((1, CH), F32),
            pltpu.VMEM((2, 49, 8, LANES), F32),
            pltpu.VMEM((FACES, 2, PADROWS * STRIDE, LANES), F32),
            pltpu.VMEM(fields.shape, F32),
            pltpu.VMEM(fields.shape, BF16),
            strip, strip,
            pltpu.VMEM((2, 2, 3, STRIP, LANES), BF16),
            corners,
            strip, strip,
            halo_rows, halo_rows,
            pltpu.VMEM((2, 2, 3, STRIP, LANES), BF16),
            corners,
            relayed,
            pltpu.VMEM((2, SIDES * FACES, 3, 8, LANES), F32),
            relayed, relayed_half, relayed_half,
            pltpu.SemaphoreType.DMA((12,)),
            pltpu.SemaphoreType.DMA((24,)),
            pltpu.SemaphoreType.DMA((11,)),
            pltpu.SemaphoreType.DMA,
        ],
        compiler_params=pltpu.CompilerParams(
            collective_id=0, has_side_effects=True, vmem_limit_bytes=63 * 2**20
        ),
        name="convnext_block",
    )(
        fields, neighbour.T, rotation.T, conv_weight, row(conv_bias), row(norm_gain), row(norm_shift),
        weight_in, row(bias_in), weight_out, row(bias_out), row(layer_scale),
    )


def solution(mesh):
    cells = P(None, "tile", "chan", None)
    return jax.shard_map(
        block, mesh=mesh, in_specs=(cells,) + (P(),) * 11, out_specs=cells, check_vma=False
    )
```

```python
import functools

import jax
import jax.numpy as jnp
from jax import lax
from jax.experimental import pallas as pl
from jax.experimental.pallas import tpu as pltpu
from jax.sharding import PartitionSpec as P

F32, BF16 = jnp.float32, jnp.bfloat16
FACES, ROWS, COLS, CH, HID = 12, 8, 16, 256, 1024
LANES = 128
TILES, CHANS = 16, 8
STRIDE = 32
FIRST = 8
PADROWS = ROWS + 6
SIDES = 4
STRIP = FACES * 8
RELAYS = (
    (106, 77, 46, 9, 98, 69, 38, 1, 122, 93, 62, 25, 114, 85, 54, 17),
    (21, 50, 81, 118, 29, 58, 89, 126, 5, 34, 65, 102, 13, 42, 73, 110),
)


def pick(values, index):
    if len(values) == 1:
        return values[0]
    low = index % 2 == 0
    return pick([jnp.where(low, a, b) for a, b in zip(values[::2], values[1::2])], index // 2)


def relay_of(block, half):
    device = pick(RELAYS[half], block)
    return {"tile": device // CHANS, "chan": device % CHANS}


def relay_role(i, j):
    device = i * CHANS + j
    place = sum(
        jnp.where(device == relay, 1 + block + 16 * half, 0)
        for half in range(2)
        for block, relay in enumerate(RELAYS[half])
    )
    return place > 0, jnp.maximum(place - 1, 0) % 16, jnp.maximum(place - 1, 0) // 16


def each_quad(body):
    lax.fori_loop(0, FACES // 4, lambda quad, c: (body(quad), c)[1], 0)


def each_pair(body):
    lax.fori_loop(0, FACES // 2, lambda pair, c: (body(pair), c)[1], 0)


def each_face(body):
    lax.fori_loop(0, FACES, lambda face, c: (body(face), c)[1], 0)


def lanes(half):
    return pl.ds(half * LANES, LANES)


def pair_rows(pair):
    return pl.ds(pl.multiple_of(pair * 16, 16), 16)


def kernel(
    fields, neighbour, rotation, conv_weight, conv_bias, norm_gain, norm_shift,
    weight_in, bias_in, weight_out, bias_out, layer_scale,
    out,
    x, nbr, rot, cw, cb, gain, shift, w_in, b_in, w_out, b_out, scale,
    taps, padded, acc, result,
    send_left, send_right, send_edge, send_corner, columns, halo_rows, seam, corner,
    relay_in, relay_all, relay_out, relay_first, relay_last,
    local_sems, send_sems, recv_sems, out_sem,
):
    i, j = lax.axis_index("tile"), lax.axis_index("chan")
    has_up, has_down = i > 0, i < TILES - 1
    has_left, has_right = j > 0, j < CHANS - 1
    is_top, is_bottom = i == 0, i == TILES - 1
    is_left, is_right = j == 0, j == CHANS - 1
    is_relay, block, my_half = relay_role(i, j)
    turned_block = 15 - block
    odd = block % 2 == 1

    locals_ = [
        pltpu.make_async_copy(src, dst, local_sems.at[n])
        for n, (src, dst) in enumerate(
            [
                (fields, x), (neighbour, nbr), (rotation, rot), (conv_weight, cw), (conv_bias, cb),
                (norm_gain, gain), (norm_shift, shift), (weight_in, w_in), (bias_in, b_in),
                (weight_out, w_out), (bias_out, b_out), (layer_scale, scale),
            ]
        )
    ]
    for copy in locals_:
        copy.start()

    barrier = pltpu.get_barrier_semaphore()

    def greet(tile, chan):
        pl.semaphore_signal(
            barrier, inc=1, device_id={"tile": tile, "chan": chan},
            device_id_type=pl.DeviceIdType.MESH,
        )

    def greet_relays(block_):
        for half in range(2):
            there = relay_of(block_, half)
            greet(there["tile"], there["chan"])

    pl.when(has_up)(lambda: greet(i - 1, j))
    pl.when(has_down)(lambda: greet(i + 1, j))
    pl.when(has_left)(lambda: greet(i, j - 1))
    pl.when(has_right)(lambda: greet(i, j + 1))
    pl.when(has_up & has_left)(lambda: greet(i - 1, j - 1))
    pl.when(has_up & has_right)(lambda: greet(i - 1, j + 1))
    pl.when(has_down & has_left)(lambda: greet(i + 1, j - 1))
    pl.when(has_down & has_right)(lambda: greet(i + 1, j + 1))

    @pl.when(is_relay)
    def _():
        greet(0, 7 - block // 2)
        greet(block, 0)
        greet(TILES - 1, block // 2)
        greet(turned_block, CHANS - 1)

    def greet_end(to_block):
        greet_relays(to_block(2 * j))
        greet_relays(to_block(2 * j + 1))
        pl.when(has_left)(lambda: greet_relays(to_block(2 * j - 1)))
        pl.when(has_right)(lambda: greet_relays(to_block(2 * j + 2)))

    def greet_side(to_block):
        greet_relays(to_block(i))
        pl.when(has_up)(lambda: greet_relays(to_block(i - 1)))
        pl.when(has_down)(lambda: greet_relays(to_block(i + 1)))

    pl.when(is_top)(lambda: greet_end(lambda t: t))
    pl.when(is_bottom)(lambda: greet_end(lambda t: 15 - t))
    pl.when(is_left)(lambda: greet_side(lambda t: 15 - t))
    pl.when(is_right)(lambda: greet_side(lambda t: t))

    def as_int(flag):
        return flag.astype(jnp.int32)

    not_first, not_last = as_int(block > 0), as_int(block < 15)
    expected = (
        (1 + as_int(has_up) + as_int(has_down)) * (1 + as_int(has_left) + as_int(has_right)) - 1
        + 4 * as_int(is_top) + 4 * as_int(is_bottom) + 2 * as_int(is_left) + 2 * as_int(is_right)
        + as_int(is_relay)
        * (4 + 2 * (not_first + not_last) + 2 * jnp.where(odd, not_last, not_first))
    )

    locals_[0].wait()

    sublane = lax.broadcasted_iota(jnp.int32, (8, LANES), 0)

    def lower_half(a, b):
        return jnp.where(sublane < 4, a, pltpu.roll(b, 4, 0))

    def upper_half(a, b):
        return jnp.where(sublane < 4, pltpu.roll(a, 4, 0), b)

    def two(a, b):
        return jnp.concatenate([a, b], axis=0).astype(BF16)

    def pack_edge(row_of):
        def body(pair):
            for half in range(2):
                for k in range(3):
                    rows = [x[2 * pair + e, row_of(k), :, lanes(half)].astype(F32) for e in range(2)]
                    for seg in range(2):
                        send_edge[seg, half, k, pair_rows(pair), :] = two(
                            *[row[8 * seg : 8 * seg + 8] for row in rows]
                        )

        each_pair(body)

    pl.when(is_top)(lambda: pack_edge(lambda k: k))
    pl.when(is_bottom)(lambda: pack_edge(lambda k: ROWS - 1 - k))

    def unpack(face):
        for half in range(2):
            for r in range(ROWS):
                padded[face, half, pl.ds((r + 3) * STRIDE + FIRST, COLS), :] = x[
                    face, r, :, lanes(half)
                ].astype(F32)
        zero = jnp.zeros((8, LANES), F32)
        for half in range(2):
            for r in (0, 1, 2, 11, 12, 13):
                padded[face, half, pl.ds(r * STRIDE, 8), :] = zero
                padded[face, half, pl.ds(r * STRIDE + FIRST + COLS, 8), :] = zero

    each_face(unpack)

    def column(face, half, first_row, c):
        return padded[face, half, pl.ds(first_row * STRIDE + c + FIRST, 8, stride=STRIDE), :]

    def pack_columns(quad):
        for half in range(2):
            for k in range(3):
                for side, (target, c) in enumerate(((send_left, k), (send_right, COLS - 1 - k))):
                    cells = [column(4 * quad + e, half, 3, c) for e in range(4)]
                    for e in range(2):
                        target[half, k, pair_rows(2 * quad + e), :] = two(*cells[2 * e : 2 * e + 2])
                    send_corner[2 * side, half, k, pair_rows(quad), :] = two(
                        lower_half(*cells[:2]), lower_half(*cells[2:])
                    )
                    send_corner[2 * side + 1, half, k, pair_rows(quad), :] = two(
                        upper_half(*cells[:2]), upper_half(*cells[2:])
                    )

    each_quad(pack_columns)

    pl.semaphore_wait(barrier, expected)

    def remote(src, dst, send, recv, where):
        return pltpu.make_async_remote_copy(
            src_ref=src, dst_ref=dst, send_sem=send_sems.at[send], recv_sem=recv_sems.at[recv],
            device_id=where, device_id_type=pl.DeviceIdType.MESH,
        )

    COLUMNS, HALO_ROWS, SEAM, CORNER, RELAY = 0, 2, 4, 5, 9

    edge_sends = [
        (is_top, [
            remote(send_edge.at[seg, half, k], relay_in.at[k, 0], 6 * k + 2 * seg + half, RELAY + k,
                   relay_of(15 - (2 * j + seg), half))
            for k in range(3) for seg in range(2) for half in range(2)
        ]),
        (is_bottom, [
            remote(send_edge.at[seg, half, k], relay_in.at[k, 2], 6 * k + 2 * seg + half, RELAY + k,
                   relay_of(2 * j + seg, half))
            for k in range(3) for seg in range(2) for half in range(2)
        ]),
        (is_left, [
            remote(send_left.at[half, k], relay_in.at[k, 1], 6 * k + 4 + half, RELAY + k,
                   relay_of(i, half))
            for k in range(3) for half in range(2)
        ]),
        (is_right, [
            remote(send_right.at[half, k], relay_in.at[k, 3], 6 * k + 4 + half, RELAY + k,
                   relay_of(15 - i, half))
            for k in range(3) for half in range(2)
        ]),
    ]
    halo_sends = [
        (has_up, [remote(x.at[:, pl.ds(0, 3)], halo_rows.at[1], 18, HALO_ROWS + 1,
                         {"tile": i - 1, "chan": j})]),
        (has_down, [remote(x.at[:, pl.ds(ROWS - 3, 3)], halo_rows.at[0], 19, HALO_ROWS,
                           {"tile": i + 1, "chan": j})]),
        (has_left, [remote(send_left, columns.at[1], 20, COLUMNS + 1, {"tile": i, "chan": j - 1})]),
        (has_right, [remote(send_right, columns.at[0], 21, COLUMNS, {"tile": i, "chan": j + 1})]),
    ]
    for side, (there, has_side) in enumerate(((j - 1, has_left), (j + 1, has_right))):
        for end, (tile, has_end) in enumerate(((i - 1, has_up), (i + 1, has_down))):
            mine, theirs = 2 * side + end, 3 - (2 * side + end)
            halo_sends.append((
                has_side & has_end,
                [remote(send_corner.at[mine], corner.at[theirs], 22 + mine, CORNER + theirs,
                        {"tile": tile, "chan": there})],
            ))

    def relay_sends(k):
        def pass_on(source, corner_at, n, tile, chan):
            return remote(source, corner.at[corner_at, my_half, k], 26 + 10 * k + n,
                          CORNER + corner_at, {"tile": tile, "chan": chan})

        def to(side, target, n, recv, tile, chan):
            return remote(relay_out.at[k, side], target, 26 + 10 * k + n, recv,
                          {"tile": tile, "chan": chan})

        first, last = relay_first.at[k], relay_last.at[k]
        return [
            (is_relay, [
                to(0, seam.at[block % 2, my_half, k], 0, SEAM, 0, block // 2),
                to(2, seam.at[turned_block % 2, my_half, k], 1, SEAM, TILES - 1, turned_block // 2),
                to(1, columns.at[0, my_half, k], 2, COLUMNS, turned_block, 0),
                to(3, columns.at[1, my_half, k], 3, COLUMNS + 1, block, CHANS - 1),
            ]),
            (is_relay & odd & (block < 15), [
                pass_on(last.at[0], 0, 4, 0, block // 2 + 1),
                pass_on(first.at[2], 3, 5, TILES - 1, turned_block // 2 - 1),
            ]),
            (is_relay & ~odd & (block > 0), [
                pass_on(first.at[0], 2, 4, 0, block // 2 - 1),
                pass_on(last.at[2], 1, 5, TILES - 1, turned_block // 2 + 1),
            ]),
            (is_relay & (turned_block < 15), [pass_on(last.at[1], 0, 6, turned_block + 1, 0)]),
            (is_relay & (turned_block > 0), [pass_on(first.at[1], 1, 7, turned_block - 1, 0)]),
            (is_relay & (block < 15), [pass_on(last.at[3], 2, 8, block + 1, CHANS - 1)]),
            (is_relay & (block > 0), [pass_on(first.at[3], 3, 9, block - 1, CHANS - 1)]),
        ]

    def start_all(sends):
        for condition, copies in sends:
            @pl.when(condition)
            def _():
                for copy in copies:
                    copy.start()

    def arrived(buffer, recv):
        pltpu.make_async_copy(buffer, buffer, recv_sems.at[recv]).wait()

    start_all(edge_sends)
    start_all(halo_sends)

    locals_[3].wait()
    locals_[4].wait()
    for half in range(2):
        for a in range(7):
            for b in range(7):
                taps[half, a * 7 + b] = jnp.broadcast_to(cw[a, pl.ds(b, 1), lanes(half)], (8, LANES))

    def convolve(face, half, group, total, rows, shifts):
        for b in shifts:
            cells = {
                r: padded[face, half, pl.ds(r * STRIDE + FIRST - 3 + b + 8 * group, 8), :]
                for r in rows
            }
            for a in range(7):
                tap = taps[half, a * 7 + b]
                for r in range(ROWS):
                    if r + a in cells and r in total:
                        total[r] = total[r] + tap * cells[r + a]
        return total

    own = range(3, 11)
    near = (range(3, 7), range(4))
    far = (range(3), range(4, 7))

    def add_taps(side, out_rows, rows, shifts, first=False):
        def body(face):
            for half in range(2):
                if first:
                    bias = jnp.broadcast_to(cb[:, lanes(half)], (8, LANES))
                    total = {r: bias for r in out_rows}
                else:
                    total = {r: acc[side, r, face, :, lanes(half)] for r in out_rows}
                for r, value in convolve(face, half, side, total, rows, shifts).items():
                    acc[side, r, face, :, lanes(half)] = value

        each_face(body)

    for side in range(2):
        add_taps(side, range(ROWS), own, near[side], first=True)

    locals_[1].wait()
    locals_[2].wait()

    @pl.when(is_relay)
    def _():
        row = lax.broadcasted_iota(jnp.int32, (STRIP, STRIP), 0)
        col = lax.broadcasted_iota(jnp.int32, (STRIP, STRIP), 1)
        turn = (row // 8 * 8 + 7 - row % 8 == col).astype(BF16)

        def relay(k, carry):
            arrived(relay_in.at[k], RELAY + k)
            for side in range(SIDES):
                strip = relay_in[k, side]
                at = pl.ds(side * FACES, FACES)
                relay_all[0, at] = strip.astype(F32).reshape(FACES, 8, LANES)
                relay_all[1, at] = jnp.dot(turn, strip, preferred_element_type=F32).reshape(
                    FACES, 8, LANES
                )

            def choose(quad):
                for side in range(SIDES):
                    cells = []
                    for e in range(4):
                        source = (side + 6 - rot[side, 4 * quad + e]) & 3
                        same = ((source + 1) & 3) >> 1
                        flip = same if side in (1, 2) else 1 - same
                        cells.append(relay_all[flip, source * FACES + nbr[side, 4 * quad + e]])
                    for e in range(2):
                        relay_out[k, side, pair_rows(2 * quad + e), :] = two(
                            *cells[2 * e : 2 * e + 2]
                        )
                    relay_first[k, side, pair_rows(quad), :] = two(
                        lower_half(*cells[:2]), lower_half(*cells[2:])
                    )
                    relay_last[k, side, pair_rows(quad), :] = two(
                        upper_half(*cells[:2]), upper_half(*cells[2:])
                    )

            each_quad(choose)
            start_all(relay_sends(k))
            return carry

        lax.fori_loop(0, 3, relay, 0)

    def unpack_rows(end, first_row):
        def body(face):
            for half in range(2):
                for r in range(3):
                    padded[face, half, pl.ds((first_row + r) * STRIDE + FIRST, COLS), :] = halo_rows[
                        end, face, r, :, lanes(half)
                    ].astype(F32)

        each_face(body)

    def unpack_seam(row_of):
        def body(pair):
            for half in range(2):
                for seg in range(2):
                    for k in range(3):
                        both = seam[seg, half, k, pair_rows(pair), :].astype(F32)
                        for e in range(2):
                            padded[
                                2 * pair + e, half, pl.ds(row_of(k) * STRIDE + FIRST + 8 * seg, 8), :
                            ] = both[8 * e : 8 * e + 8]

        each_pair(body)

    def unpack_columns(side):
        def body(pair):
            for half in range(2):
                for k in range(3):
                    both = columns[side, half, k, pair_rows(pair), :].astype(F32)
                    col = -1 - k if side == 0 else COLS + k
                    for e in range(2):
                        padded[
                            2 * pair + e, half,
                            pl.ds(3 * STRIDE + FIRST + col, 8, stride=STRIDE), :
                        ] = both[8 * e : 8 * e + 8]

        each_pair(body)

    def unpack_corner(at, beside, end):
        first_col = -4 if at < 2 else COLS

        def body(quad):
            for half in range(2):
                for k in range(3):
                    cells = corner[at, half, k, pair_rows(quad), :].astype(F32)
                    for e in range(4):
                        if beside:
                            col = -1 - k if at < 2 else COLS + k
                            first, row = (1, 0) if end == 0 else (0, 11)
                            padded[
                                4 * quad + e, half,
                                pl.ds(row * STRIDE + FIRST + col, 3, stride=STRIDE), :
                            ] = cells[4 * e + first : 4 * e + first + 3]
                        else:
                            row = 2 - k if end == 0 else 11 + k
                            padded[
                                4 * quad + e, half, pl.ds(row * STRIDE + FIRST + first_col, 4), :
                            ] = cells[4 * e : 4 * e + 4]

        each_quad(body)

    by_columns = is_left | is_right
    late = (is_left, is_right)
    first_end = as_int(is_top)

    def take_rows(end):
        at_end = (is_top, is_bottom)[end]

        @pl.when(~at_end)
        def _():
            arrived(halo_rows.at[end], HALO_ROWS + end)
            unpack_rows(end, 11 * end)

        @pl.when(at_end)
        def _():
            arrived(seam, SEAM)
            unpack_seam((lambda k: 2 - k) if end == 0 else (lambda k: 11 + k))

    def take_columns(side):
        arrived(columns.at[side], COLUMNS + side)
        unpack_columns(side)
        add_taps(side, range(ROWS), own, far[side])

    def take_corner(end, side):
        at = 2 * side + end
        has_side, has_end = (has_left, has_right)[side], (has_up, has_down)[end]

        @pl.when(has_side | has_end)
        def _():
            arrived(corner.at[at], CORNER + at)

        pl.when(has_end)(functools.partial(unpack_corner, at, True, end))
        pl.when(~has_end & has_side)(functools.partial(unpack_corner, at, False, end))

    def add_end(end, side, shifts):
        if end == 0:
            add_taps(side, range(3), range(3), shifts)
        else:
            add_taps(side, range(5, 8), range(11, 14), shifts)

    for copy in locals_[5:]:
        copy.wait()

    def pointwise(at):
        cells = acc.at[at]
        shape = cells.shape
        values = cells[...].reshape(-1, CH).astype(BF16).astype(F32)
        mean = jnp.mean(values, axis=-1, keepdims=True)
        apart = values - mean
        spread = jnp.mean(apart * apart, axis=-1, keepdims=True)
        normed = (apart * lax.rsqrt(spread + 1e-6) * gain[...] + shift[...]).astype(BF16)
        hidden = jnp.dot(normed, w_in[...], preferred_element_type=F32) + b_in[...]
        inner_ = hidden * (0.7978845608028654 + 0.035677408136300125 * (hidden * hidden))
        hidden = (hidden * (1.0 + jnp.tanh(inner_))).astype(BF16)
        update = 0.5 * jnp.dot(hidden, w_out[...], preferred_element_type=F32) + b_out[...]
        cells[...] = (scale[...] * update).reshape(shape)

    def finish(first, count):
        def body(face):
            for r in range(count):
                row = first + r
                for half in range(2):
                    update = jnp.concatenate(
                        [acc[side, row, face, :, lanes(half)] for side in range(2)], axis=0
                    )
                    result[face, row, :, lanes(half)] = (
                        x[face, row, :, lanes(half)].astype(F32) + update
                    ).astype(BF16)
            rows = pl.ds(first, count)
            pltpu.make_async_copy(result.at[face, rows], out.at[face, rows], out_sem).start()

        each_face(body)

    both = pl.ds(0, 2)
    early_side = as_int(is_left)

    for side in range(2):
        pl.when(~late[side])(functools.partial(take_columns, side))

    @pl.when(~by_columns)
    def _():
        pointwise((both, pl.ds(3, 2)))
        finish(3, 2)

    def take_end(n, carry):
        end = (first_end + n) % 2
        for an_end in range(2):
            @pl.when(end == an_end)
            def _():
                take_rows(an_end)
                for side in range(2):
                    @pl.when(~late[side])
                    def _():
                        take_corner(an_end, side)
                        add_end(an_end, side, range(7))

                    @pl.when(late[side])
                    def _():
                        add_end(an_end, side, near[side])

        @pl.when(~by_columns)
        def _():
            pointwise((both, pl.ds(5 * end, 3)))
            finish(5 * end, 3)

        @pl.when(by_columns)
        def _():
            pointwise((early_side, pl.ds(4 * end, 4)))

        return carry

    lax.fori_loop(0, 2, take_end, 0)

    for side in range(2):
        @pl.when(late[side])
        def _():
            take_columns(side)
            for end in range(2):
                take_corner(end, side)
                add_end(end, side, far[side])

    @pl.when(by_columns)
    def _():
        def last(end, carry):
            pointwise((1 - early_side, pl.ds(4 * end, 4)))
            finish(4 * end, 4)
            return carry

        lax.fori_loop(0, 2, last, 0)

    pltpu.make_async_copy(result, out, out_sem).wait()

    for condition, copies in edge_sends + halo_sends:
        @pl.when(condition)
        def _():
            for copy in copies:
                copy.wait_send()

    for k in range(3):
        for condition, copies in relay_sends(k):
            @pl.when(condition)
            def _():
                for copy in copies:
                    copy.wait_send()


def block(fields, neighbour, rotation, conv_weight, conv_bias, norm_gain, norm_shift,
          weight_in, bias_in, weight_out, bias_out, layer_scale):
    def row(vector):
        return vector.reshape(1, -1)

    anywhere = pl.BlockSpec(memory_space=pl.ANY)
    strip = pltpu.VMEM((2, 3, STRIP, LANES), BF16)
    corners = pltpu.VMEM((4, 2, 3, STRIP // 2, LANES), BF16)
    relayed = pltpu.VMEM((3, SIDES, STRIP, LANES), BF16)
    relayed_half = pltpu.VMEM((3, SIDES, STRIP // 2, LANES), BF16)
    return pl.pallas_call(
        kernel,
        out_shape=jax.ShapeDtypeStruct(fields.shape, BF16),
        in_specs=[anywhere] * 12,
        out_specs=anywhere,
        scratch_shapes=[
            pltpu.VMEM(fields.shape, BF16),
            pltpu.SMEM((SIDES, FACES), jnp.int32),
            pltpu.SMEM((SIDES, FACES), jnp.int32),
            pltpu.VMEM((7, 7, CH), F32),
            pltpu.VMEM((1, CH), F32),
            pltpu.VMEM((1, CH), F32),
            pltpu.VMEM((1, CH), F32),
            pltpu.VMEM((CH, HID), BF16),
            pltpu.VMEM((1, HID), F32),
            pltpu.VMEM((HID, CH), BF16),
            pltpu.VMEM((1, CH), F32),
            pltpu.VMEM((1, CH), F32),
            pltpu.VMEM((2, 49, 8, LANES), F32),
            pltpu.VMEM((FACES, 2, PADROWS * STRIDE, LANES), F32),
            pltpu.VMEM((2, ROWS, FACES, 8, CH), F32),
            pltpu.VMEM(fields.shape, BF16),
            strip, strip,
            pltpu.VMEM((2, 2, 3, STRIP, LANES), BF16),
            corners,
            pltpu.VMEM((2, 2, 3, STRIP, LANES), BF16),
            pltpu.VMEM((2, FACES, 3, COLS, CH), BF16),
            pltpu.VMEM((2, 2, 3, STRIP, LANES), BF16),
            corners,
            relayed,
            pltpu.VMEM((2, SIDES * FACES, 8, LANES), F32),
            relayed, relayed_half, relayed_half,
            pltpu.SemaphoreType.DMA((12,)),
            pltpu.SemaphoreType.DMA((56,)),
            pltpu.SemaphoreType.DMA((12,)),
            pltpu.SemaphoreType.DMA,
        ],
        compiler_params=pltpu.CompilerParams(
            collective_id=0, has_side_effects=True, vmem_limit_bytes=63 * 2**20
        ),
        name="convnext_block",
    )(
        fields, neighbour.T, rotation.T, conv_weight, row(conv_bias), row(norm_gain), row(norm_shift),
        weight_in, row(bias_in), weight_out, row(bias_out), row(layer_scale),
    )


def solution(mesh):
    cells = P(None, "tile", "chan", None)
    return jax.shard_map(
        block, mesh=mesh, in_specs=(cells,) + (P(),) * 11, out_specs=cells, check_vma=False
    )
```

```python
import functools

import jax
import jax.numpy as jnp
from jax import lax
from jax.experimental import pallas as pl
from jax.experimental.pallas import tpu as pltpu
from jax.sharding import PartitionSpec as P

F32, BF16 = jnp.float32, jnp.bfloat16
FACES, ROWS, COLS, CH, HID = 12, 8, 16, 256, 1024
LANES = 128
TILES, CHANS = 16, 8
STRIDE = 32
FIRST = 8
PADROWS = ROWS + 6
SIDES = 4
STRIP = FACES * 8
RELAYS = (
    (25, 106, 9, 102, 36, 58, 105, 92, 90, 84, 50, 28, 14, 113, 118, 101),
    (70, 22, 114, 62, 100, 66, 12, 65, 34, 10, 20, 38, 30, 17, 97, 57),
)


def pick(values, index):
    if len(values) == 1:
        return values[0]
    low = index % 2 == 0
    return pick([jnp.where(low, a, b) for a, b in zip(values[::2], values[1::2])], index // 2)


def relay_of(block, half):
    device = pick(RELAYS[half], block)
    return {"tile": device // CHANS, "chan": device % CHANS}


def relay_role(i, j):
    device = i * CHANS + j
    place = sum(
        jnp.where(device == relay, 1 + block + 16 * half, 0)
        for half in range(2)
        for block, relay in enumerate(RELAYS[half])
    )
    return place > 0, jnp.maximum(place - 1, 0) % 16, jnp.maximum(place - 1, 0) // 16


def each_quad(body):
    lax.fori_loop(0, FACES // 4, lambda quad, c: (body(quad), c)[1], 0)


def each_pair(body):
    lax.fori_loop(0, FACES // 2, lambda pair, c: (body(pair), c)[1], 0)


def each_face(body):
    lax.fori_loop(0, FACES, lambda face, c: (body(face), c)[1], 0)


def lanes(half):
    return pl.ds(half * LANES, LANES)


def pair_rows(pair):
    return pl.ds(pl.multiple_of(pair * 16, 16), 16)


def kernel(
    fields, neighbour, rotation, conv_weight, conv_bias, norm_gain, norm_shift,
    weight_in, bias_in, weight_out, bias_out, layer_scale,
    out,
    x, nbr, rot, cw, cb, gain, shift, w_in, b_in, w_out, b_out, scale,
    taps, padded, acc, kept, patch, result,
    send_left, send_right, send_edge, send_ends, columns, halo_rows, seam, corner, ends_in,
    relay_in, relay_all, relay_out, relay_first, relay_last,
    local_sems, send_sems, recv_sems, out_sem,
):
    i, j = lax.axis_index("tile"), lax.axis_index("chan")
    has_up, has_down = i > 0, i < TILES - 1
    has_left, has_right = j > 0, j < CHANS - 1
    is_top, is_bottom = i == 0, i == TILES - 1
    is_left, is_right = j == 0, j == CHANS - 1
    is_relay, block, my_half = relay_role(i, j)
    turned_block = 15 - block
    odd = block % 2 == 1

    locals_ = [
        pltpu.make_async_copy(src, dst, local_sems.at[n])
        for n, (src, dst) in enumerate(
            [
                (fields, x), (neighbour, nbr), (rotation, rot), (conv_weight, cw), (conv_bias, cb),
                (norm_gain, gain), (norm_shift, shift), (weight_in, w_in), (bias_in, b_in),
                (weight_out, w_out), (bias_out, b_out), (layer_scale, scale),
            ]
        )
    ]
    locals_[0].start()

    barrier = pltpu.get_barrier_semaphore()

    def greet(tile, chan):
        pl.semaphore_signal(
            barrier, inc=1, device_id={"tile": tile, "chan": chan},
            device_id_type=pl.DeviceIdType.MESH,
        )

    def greet_relays(block_):
        for half in range(2):
            there = relay_of(block_, half)
            greet(there["tile"], there["chan"])

    @pl.when(is_relay)
    def _():
        greet(0, 7 - block // 2)
        greet(block, 0)
        greet(TILES - 1, block // 2)
        greet(turned_block, CHANS - 1)

    def greet_end(to_block):
        greet_relays(to_block(2 * j))
        greet_relays(to_block(2 * j + 1))
        pl.when(has_left)(lambda: greet_relays(to_block(2 * j - 1)))
        pl.when(has_right)(lambda: greet_relays(to_block(2 * j + 2)))

    def greet_side(to_block):
        greet_relays(to_block(i))
        pl.when(has_up)(lambda: greet_relays(to_block(i - 1)))
        pl.when(has_down)(lambda: greet_relays(to_block(i + 1)))

    pl.when(is_top)(lambda: greet_end(lambda t: t))
    pl.when(is_bottom)(lambda: greet_end(lambda t: 15 - t))
    pl.when(is_left)(lambda: greet_side(lambda t: 15 - t))
    pl.when(is_right)(lambda: greet_side(lambda t: t))

    pl.when(has_up)(lambda: greet(i - 1, j))
    pl.when(has_down)(lambda: greet(i + 1, j))
    pl.when(has_left)(lambda: greet(i, j - 1))
    pl.when(has_right)(lambda: greet(i, j + 1))
    for copy in locals_[1:]:
        copy.start()

    def as_int(flag):
        return flag.astype(jnp.int32)

    not_first, not_last = as_int(block > 0), as_int(block < 15)
    expected = (
        as_int(has_up) + as_int(has_down) + as_int(has_left) + as_int(has_right)
        + 4 * as_int(is_top) + 4 * as_int(is_bottom) + 2 * as_int(is_left) + 2 * as_int(is_right)
        + as_int(is_relay)
        * (4 + 2 * (not_first + not_last) + 2 * jnp.where(odd, not_last, not_first))
    )

    locals_[0].wait()

    sublane = lax.broadcasted_iota(jnp.int32, (8, LANES), 0)

    def lower_half(a, b):
        return jnp.where(sublane < 4, a, pltpu.roll(b, 4, 0))

    def upper_half(a, b):
        return jnp.where(sublane < 4, pltpu.roll(a, 4, 0), b)

    def two(a, b):
        return jnp.concatenate([a, b], axis=0).astype(BF16)

    def pack_edge(row_of):
        def body(pair):
            for half in range(2):
                for k in range(3):
                    rows = [x[2 * pair + e, row_of(k), :, lanes(half)].astype(F32) for e in range(2)]
                    for seg in range(2):
                        send_edge[seg, half, k, pair_rows(pair), :] = two(
                            *[row[8 * seg : 8 * seg + 8] for row in rows]
                        )

        each_pair(body)

    pl.when(is_top)(lambda: pack_edge(lambda k: k))
    pl.when(is_bottom)(lambda: pack_edge(lambda k: ROWS - 1 - k))

    def unpack(face):
        for half in range(2):
            for r in range(ROWS):
                padded[face, half, pl.ds((r + 3) * STRIDE + FIRST, COLS), :] = x[
                    face, r, :, lanes(half)
                ].astype(F32)
        zero = jnp.zeros((8, LANES), F32)
        for half in range(2):
            for r in (0, 1, 2, 11, 12, 13):
                padded[face, half, pl.ds(r * STRIDE, 8), :] = zero
                padded[face, half, pl.ds(r * STRIDE + FIRST + COLS, 8), :] = zero

    each_face(unpack)

    @pl.when(is_left | is_right)
    def _():
        def clear(face):
            for half in range(2):
                for r in range(3, 11):
                    for c in (-FIRST, COLS):
                        padded[face, half, pl.ds(r * STRIDE + FIRST + c, 8), :] = jnp.zeros(
                            (8, LANES), F32
                        )

        each_face(clear)

    def column(face, half, first_row, c):
        return padded[face, half, pl.ds(first_row * STRIDE + c + FIRST, 8, stride=STRIDE), :]

    def pack_columns(quad):
        for half in range(2):
            for k in range(3):
                for target, c in ((send_left, k), (send_right, COLS - 1 - k)):
                    cells = [column(4 * quad + e, half, 3, c) for e in range(4)]
                    for e in range(2):
                        target[half, k, pair_rows(2 * quad + e), :] = two(*cells[2 * e : 2 * e + 2])

    each_quad(pack_columns)

    pl.semaphore_wait(barrier, expected)

    def remote(src, dst, send, recv, where):
        return pltpu.make_async_remote_copy(
            src_ref=src, dst_ref=dst, send_sem=send_sems.at[send], recv_sem=recv_sems.at[recv],
            device_id=where, device_id_type=pl.DeviceIdType.MESH,
        )

    COLUMNS, HALO_ROWS, SEAM, CORNER, RELAY, ENDS = 0, 2, 4, 5, 9, 12

    edge_sends = [
        (is_top, [
            remote(send_edge.at[seg, half, k], relay_in.at[k, 0], 6 * k + 2 * seg + half, RELAY + k,
                   relay_of(15 - (2 * j + seg), half))
            for k in range(3) for seg in range(2) for half in range(2)
        ]),
        (is_bottom, [
            remote(send_edge.at[seg, half, k], relay_in.at[k, 2], 6 * k + 2 * seg + half, RELAY + k,
                   relay_of(2 * j + seg, half))
            for k in range(3) for seg in range(2) for half in range(2)
        ]),
        (is_left, [
            remote(send_left.at[half, k], relay_in.at[k, 1], 6 * k + 4 + half, RELAY + k,
                   relay_of(i, half))
            for k in range(3) for half in range(2)
        ]),
        (is_right, [
            remote(send_right.at[half, k], relay_in.at[k, 3], 6 * k + 4 + half, RELAY + k,
                   relay_of(15 - i, half))
            for k in range(3) for half in range(2)
        ]),
    ]
    halo_sends = [
        (has_up, [remote(x.at[:, pl.ds(0, 3)], halo_rows.at[1], 18, HALO_ROWS + 1,
                         {"tile": i - 1, "chan": j})]),
        (has_down, [remote(x.at[:, pl.ds(ROWS - 3, 3)], halo_rows.at[0], 19, HALO_ROWS,
                           {"tile": i + 1, "chan": j})]),
        (has_left, [remote(send_left, columns.at[1], 20, COLUMNS + 1, {"tile": i, "chan": j - 1})]),
        (has_right, [remote(send_right, columns.at[0], 21, COLUMNS, {"tile": i, "chan": j + 1})]),
    ]
    end_sends = [
        (has_left, [remote(send_ends.at[0], ends_in.at[1], 22, ENDS + 1, {"tile": i, "chan": j - 1})]),
        (has_right, [remote(send_ends.at[1], ends_in.at[0], 23, ENDS, {"tile": i, "chan": j + 1})]),
    ]

    def relay_sends(k):
        def pass_on(source, corner_at, n, tile, chan):
            return remote(source, corner.at[corner_at, my_half, k], 24 + 10 * k + n,
                          CORNER + corner_at, {"tile": tile, "chan": chan})

        def to(side, target, n, recv, tile, chan):
            return remote(relay_out.at[k, side], target, 24 + 10 * k + n, recv,
                          {"tile": tile, "chan": chan})

        first, last = relay_first.at[k], relay_last.at[k]
        return [
            (is_relay, [
                to(0, seam.at[block % 2, my_half, k], 0, SEAM, 0, block // 2),
                to(2, seam.at[turned_block % 2, my_half, k], 1, SEAM, TILES - 1, turned_block // 2),
                to(1, columns.at[0, my_half, k], 2, COLUMNS, turned_block, 0),
                to(3, columns.at[1, my_half, k], 3, COLUMNS + 1, block, CHANS - 1),
            ]),
            (is_relay & odd & (block < 15), [
                pass_on(last.at[0], 0, 4, 0, block // 2 + 1),
                pass_on(first.at[2], 3, 5, TILES - 1, turned_block // 2 - 1),
            ]),
            (is_relay & ~odd & (block > 0), [
                pass_on(first.at[0], 2, 4, 0, block // 2 - 1),
                pass_on(last.at[2], 1, 5, TILES - 1, turned_block // 2 + 1),
            ]),
            (is_relay & (turned_block < 15), [pass_on(last.at[1], 0, 6, turned_block + 1, 0)]),
            (is_relay & (turned_block > 0), [pass_on(first.at[1], 1, 7, turned_block - 1, 0)]),
            (is_relay & (block < 15), [pass_on(last.at[3], 2, 8, block + 1, CHANS - 1)]),
            (is_relay & (block > 0), [pass_on(first.at[3], 3, 9, block - 1, CHANS - 1)]),
        ]

    def start_all(sends):
        for condition, copies in sends:
            @pl.when(condition)
            def _():
                for copy in copies:
                    copy.start()

    def arrived(buffer, recv):
        pltpu.make_async_copy(buffer, buffer, recv_sems.at[recv]).wait()

    start_all(edge_sends)
    start_all(halo_sends)

    locals_[3].wait()
    locals_[4].wait()
    for half in range(2):
        for a in range(7):
            for b in range(7):
                taps[half, a * 7 + b] = jnp.broadcast_to(cw[a, pl.ds(b, 1), lanes(half)], (8, LANES))

    def convolve(face, half, group, total, rows, shifts):
        for b in shifts:
            cells = {
                r: padded[face, half, pl.ds(r * STRIDE + FIRST - 3 + b + 8 * group, 8), :]
                for r in rows
            }
            for a in range(7):
                tap = taps[half, a * 7 + b]
                for r in range(ROWS):
                    if r + a in cells and r in total:
                        total[r] = total[r] + tap * cells[r + a]
        return total

    own = range(3, 11)
    near = (range(3, 7), range(4))
    far = (range(3), range(4, 7))

    def add_taps(side, out_rows, rows, shifts, first=False):
        def body(face):
            for half in range(2):
                if first:
                    bias = jnp.broadcast_to(cb[:, lanes(half)], (8, LANES))
                    total = {r: bias for r in out_rows}
                else:
                    total = {r: acc[side, r, face, :, lanes(half)] for r in out_rows}
                for r, value in convolve(face, half, side, total, rows, shifts).items():
                    acc[side, r, face, :, lanes(half)] = value

        each_face(body)

    for side in range(2):
        add_taps(side, range(ROWS), own, near[side], first=True)

    def unpack_rows(end, first_row):
        def body(face):
            for half in range(2):
                for r in range(3):
                    padded[face, half, pl.ds((first_row + r) * STRIDE + FIRST, COLS), :] = halo_rows[
                        end, face, r, :, lanes(half)
                    ].astype(F32)

        each_face(body)

    def unpack_seam(row_of):
        def body(pair):
            for half in range(2):
                for seg in range(2):
                    for k in range(3):
                        both = seam[seg, half, k, pair_rows(pair), :].astype(F32)
                        for e in range(2):
                            padded[
                                2 * pair + e, half, pl.ds(row_of(k) * STRIDE + FIRST + 8 * seg, 8), :
                            ] = both[8 * e : 8 * e + 8]

        each_pair(body)

    def unpack_columns(side):
        def body(pair):
            for half in range(2):
                for k in range(3):
                    both = columns[side, half, k, pair_rows(pair), :].astype(F32)
                    col = -1 - k if side == 0 else COLS + k
                    for e in range(2):
                        padded[
                            2 * pair + e, half,
                            pl.ds(3 * STRIDE + FIRST + col, 8, stride=STRIDE), :
                        ] = both[8 * e : 8 * e + 8]

        each_pair(body)

    def unpack_corner(at, beside, end):
        first_col = -4 if at < 2 else COLS

        def body(quad):
            for half in range(2):
                for k in range(3):
                    cells = corner[at, half, k, pair_rows(quad), :].astype(F32)
                    for e in range(4):
                        if beside:
                            col = -1 - k if at < 2 else COLS + k
                            first, row = (1, 0) if end == 0 else (0, 11)
                            padded[
                                4 * quad + e, half,
                                pl.ds(row * STRIDE + FIRST + col, 3, stride=STRIDE), :
                            ] = cells[4 * e + first : 4 * e + first + 3]
                        else:
                            row = 2 - k if end == 0 else 11 + k
                            padded[
                                4 * quad + e, half, pl.ds(row * STRIDE + FIRST + first_col, 4), :
                            ] = cells[4 * e : 4 * e + 4]

        each_quad(body)

    late = (is_left, is_right)
    any_late = is_left | is_right
    first_end = as_int(is_top)

    def take_rows(end):
        arrived(halo_rows.at[end], HALO_ROWS + end)
        unpack_rows(end, 11 * end)

    def take_seam(end):
        arrived(seam, SEAM)
        unpack_seam((lambda k: 2 - k) if end == 0 else (lambda k: 11 + k))

    def pack_ends(quad):
        for half in range(2):
            for k in range(3):
                for side in range(2):
                    c = k if side == 0 else COLS - 1 - k
                    cells = [
                        jnp.where(
                            sublane < 4,
                            column(4 * quad + e, half, 0, c),
                            column(4 * quad + e, half, 6, c),
                        )
                        for e in range(4)
                    ]
                    for e in range(2):
                        send_ends[side, half, k, pair_rows(2 * quad + e), :] = two(
                            *cells[2 * e : 2 * e + 2]
                        )

    def unpack_ends(side, end):
        def body(pair):
            for half in range(2):
                for k in range(3):
                    cells = ends_in[side, half, k, pair_rows(pair), :].astype(F32)
                    col = -1 - k if side == 0 else COLS + k
                    for e in range(2):
                        first = 8 * e + 5 * end
                        padded[
                            2 * pair + e, half,
                            pl.ds(11 * end * STRIDE + FIRST + col, 3, stride=STRIDE), :
                        ] = cells[first : first + 3]

        each_pair(body)

    def take_columns(side):
        arrived(columns.at[side], COLUMNS + side)
        unpack_columns(side)

    def take_corner(end, side, beside):
        at = 2 * side + end
        arrived(corner.at[at], CORNER + at)
        unpack_corner(at, beside, end)

    def add_end(end, side, shifts):
        if end == 0:
            add_taps(side, range(3), range(3), shifts)
        else:
            add_taps(side, range(5, 8), range(11, 14), shifts)

    for copy in locals_[5:]:
        copy.wait()

    def pointwise(cells):
        shape = cells.shape
        values = cells[...].reshape(-1, CH).astype(BF16).astype(F32)
        mean = jnp.mean(values, axis=-1, keepdims=True)
        apart = values - mean
        spread = jnp.mean(apart * apart, axis=-1, keepdims=True)
        normed = (apart * lax.rsqrt(spread + 1e-6) * gain[...] + shift[...]).astype(BF16)
        hidden = jnp.dot(normed, w_in[...], preferred_element_type=F32) + b_in[...]
        inner_ = hidden * (0.7978845608028654 + 0.035677408136300125 * (hidden * hidden))
        hidden = (hidden * (1.0 + jnp.tanh(inner_))).astype(BF16)
        update = 0.5 * jnp.dot(hidden, w_out[...], preferred_element_type=F32) + b_out[...]
        cells[...] = (scale[...] * update).reshape(shape)

    def finish(first, count):
        def body(face):
            for r in range(count):
                row = first + r
                for half in range(2):
                    update = jnp.concatenate(
                        [acc[side, row, face, :, lanes(half)] for side in range(2)], axis=0
                    )
                    result[face, row, :, lanes(half)] = (
                        x[face, row, :, lanes(half)].astype(F32) + update
                    ).astype(BF16)
            rows = pl.ds(first, count)
            pltpu.make_async_copy(result.at[face, rows], out.at[face, rows], out_sem).start()

        each_face(body)

    def keep(side, rows):
        def body(face):
            for r in rows:
                for half in range(2):
                    kept[half, face, pl.ds(8 * r, 8), :] = acc[side, r, face, :, lanes(half)]

        each_face(body)

    both = pl.ds(0, 2)

    for side in range(2):
        pl.when(~late[side])(functools.partial(take_columns, side))
        add_taps(side, range(ROWS), own, far[side])

    locals_[1].wait()
    locals_[2].wait()

    @pl.when(is_relay)
    def _():
        row = lax.broadcasted_iota(jnp.int32, (STRIP, STRIP), 0)
        col = lax.broadcasted_iota(jnp.int32, (STRIP, STRIP), 1)
        turn = (row // 8 * 8 + 7 - row % 8 == col).astype(BF16)

        def relay(k, carry):
            arrived(relay_in.at[k], RELAY + k)
            for side in range(SIDES):
                strip = relay_in[k, side]
                at = pl.ds(side * FACES, FACES)
                relay_all[0, at] = strip.astype(F32).reshape(FACES, 8, LANES)
                relay_all[1, at] = jnp.dot(turn, strip, preferred_element_type=F32).reshape(
                    FACES, 8, LANES
                )

            def choose(quad):
                for side in range(SIDES):
                    cells = []
                    for e in range(4):
                        source = (side + 6 - rot[side, 4 * quad + e]) & 3
                        same = ((source + 1) & 3) >> 1
                        flip = same if side in (1, 2) else 1 - same
                        cells.append(relay_all[flip, source * FACES + nbr[side, 4 * quad + e]])
                    for e in range(2):
                        relay_out[k, side, pair_rows(2 * quad + e), :] = two(
                            *cells[2 * e : 2 * e + 2]
                        )
                    relay_first[k, side, pair_rows(quad), :] = two(
                        lower_half(*cells[:2]), lower_half(*cells[2:])
                    )
                    relay_last[k, side, pair_rows(quad), :] = two(
                        upper_half(*cells[:2]), upper_half(*cells[2:])
                    )

            each_quad(choose)
            start_all(relay_sends(k))
            return carry

        lax.fori_loop(0, 3, relay, 0)

    for side in range(2):
        pl.when(late[side])(functools.partial(keep, side, range(3, 5)))
    pointwise(acc.at[both, pl.ds(3, 2)])
    pl.when(~any_late)(functools.partial(finish, 3, 2))

    for end in range(2):
        pl.when((has_up, has_down)[end])(functools.partial(take_rows, end))
    each_quad(pack_ends)
    start_all(end_sends)
    for end in range(2):
        @pl.when((has_up, has_down)[end])
        def _():
            for side in range(2):
                add_end(end, side, near[side])

    for side in range(2):
        @pl.when((has_left, has_right)[side])
        def _():
            arrived(ends_in.at[side], ENDS + side)
            for end in range(2):
                pl.when((has_up, has_down)[end])(functools.partial(unpack_ends, side, end))

    def take_end(n, carry):
        end = (first_end + n) % 2
        for an_end in range(2):
            at_end = (is_top, is_bottom)[an_end]

            @pl.when((end == an_end) & ~at_end)
            def _():
                for side in range(2):
                    add_end(an_end, side, far[side])

            @pl.when((end == an_end) & at_end)
            def _():
                take_seam(an_end)
                for side in range(2):
                    pl.when((has_left, has_right)[side])(
                        functools.partial(take_corner, an_end, side, False)
                    )
                    add_end(an_end, side, range(7))

            @pl.when(end == an_end)
            def _():
                for side in range(2):
                    pl.when(late[side])(
                        functools.partial(keep, side, range(3) if an_end == 0 else range(5, 8))
                    )

        pointwise(acc.at[both, pl.ds(5 * end, 3)])
        pl.when(~any_late)(lambda: finish(5 * end, 3))
        return carry

    lax.fori_loop(0, 2, take_end, 0)

    def add_columns(side):
        def body(face):
            for half in range(2):
                cells = [
                    [column(face, half, a, -1 - k if side == 0 else COLS + k) for a in range(7)]
                    for k in range(3)
                ]
                for n in range(3):
                    c = n if side == 0 else 5 + n
                    total = kept[half, face, pl.ds(c, ROWS, stride=8), :]
                    for b in range(3 - n) if side == 0 else range(6 - n, 7):
                        k = 2 - b - n if side == 0 else n + b - 6
                        for a in range(7):
                            total = total + taps[half, a * 7 + b] * cells[k][a]
                    patch[n, face, :, lanes(half)] = total

        each_face(body)

    def put_columns(side):
        def body(face):
            for half in range(2):
                for n in range(3):
                    c = n if side == 0 else 5 + n
                    kept[half, face, pl.ds(c, ROWS, stride=8), :] = patch[n, face, :, lanes(half)]
            near_seam = sublane < 3 if side == 0 else sublane > 4
            for row in range(ROWS):
                for half in range(2):
                    update = [acc[a_side, row, face, :, lanes(half)] for a_side in range(2)]
                    update[side] = jnp.where(
                        near_seam, kept[half, face, pl.ds(8 * row, 8), :], update[side]
                    )
                    result[face, row, :, lanes(half)] = (
                        x[face, row, :, lanes(half)].astype(F32) + jnp.concatenate(update, axis=0)
                    ).astype(BF16)
            pltpu.make_async_copy(result.at[face], out.at[face], out_sem).start()

        each_face(body)

    for side in range(2):
        @pl.when(late[side])
        def _():
            take_columns(side)
            for end in range(2):
                pl.when((has_up, has_down)[end])(functools.partial(take_corner, end, side, True))
            add_columns(side)

    @pl.when(any_late)
    def _():
        pointwise(patch)

    for side in range(2):
        pl.when(late[side])(functools.partial(put_columns, side))

    pltpu.make_async_copy(result, out, out_sem).wait()

    for condition, copies in edge_sends + halo_sends + end_sends:
        @pl.when(condition)
        def _():
            for copy in copies:
                copy.wait_send()

    for k in range(3):
        for condition, copies in relay_sends(k):
            @pl.when(condition)
            def _():
                for copy in copies:
                    copy.wait_send()


def block(fields, neighbour, rotation, conv_weight, conv_bias, norm_gain, norm_shift,
          weight_in, bias_in, weight_out, bias_out, layer_scale):
    def row(vector):
        return vector.reshape(1, -1)

    anywhere = pl.BlockSpec(memory_space=pl.ANY)
    strip = pltpu.VMEM((2, 3, STRIP, LANES), BF16)
    corners = pltpu.VMEM((4, 2, 3, STRIP // 2, LANES), BF16)
    relayed = pltpu.VMEM((3, SIDES, STRIP, LANES), BF16)
    relayed_half = pltpu.VMEM((3, SIDES, STRIP // 2, LANES), BF16)
    return pl.pallas_call(
        kernel,
        out_shape=jax.ShapeDtypeStruct(fields.shape, BF16),
        in_specs=[anywhere] * 12,
        out_specs=anywhere,
        scratch_shapes=[
            pltpu.VMEM(fields.shape, BF16),
            pltpu.SMEM((SIDES, FACES), jnp.int32),
            pltpu.SMEM((SIDES, FACES), jnp.int32),
            pltpu.VMEM((7, 7, CH), F32),
            pltpu.VMEM((1, CH), F32),
            pltpu.VMEM((1, CH), F32),
            pltpu.VMEM((1, CH), F32),
            pltpu.VMEM((CH, HID), BF16),
            pltpu.VMEM((1, HID), F32),
            pltpu.VMEM((HID, CH), BF16),
            pltpu.VMEM((1, CH), F32),
            pltpu.VMEM((1, CH), F32),
            pltpu.VMEM((2, 49, 8, LANES), F32),
            pltpu.VMEM((FACES, 2, PADROWS * STRIDE, LANES), F32),
            pltpu.VMEM((2, ROWS, FACES, 8, CH), F32),
            pltpu.VMEM((2, FACES, 8 * ROWS, LANES), F32),
            pltpu.VMEM((3, FACES, ROWS, CH), F32),
            pltpu.VMEM(fields.shape, BF16),
            strip, strip,
            pltpu.VMEM((2, 2, 3, STRIP, LANES), BF16),
            pltpu.VMEM((2, 2, 3, STRIP, LANES), BF16),
            pltpu.VMEM((2, 2, 3, STRIP, LANES), BF16),
            pltpu.VMEM((2, FACES, 3, COLS, CH), BF16),
            pltpu.VMEM((2, 2, 3, STRIP, LANES), BF16),
            corners,
            pltpu.VMEM((2, 2, 3, STRIP, LANES), BF16),
            relayed,
            pltpu.VMEM((2, SIDES * FACES, 8, LANES), F32),
            relayed, relayed_half, relayed_half,
            pltpu.SemaphoreType.DMA((12,)),
            pltpu.SemaphoreType.DMA((54,)),
            pltpu.SemaphoreType.DMA((14,)),
            pltpu.SemaphoreType.DMA,
        ],
        compiler_params=pltpu.CompilerParams(
            collective_id=0, has_side_effects=True, vmem_limit_bytes=63 * 2**20
        ),
        name="convnext_block",
    )(
        fields, neighbour.T, rotation.T, conv_weight, row(conv_bias), row(norm_gain), row(norm_shift),
        weight_in, row(bias_in), weight_out, row(bias_out), row(layer_scale),
    )


def solution(mesh):
    cells = P(None, "tile", "chan", None)
    return jax.shard_map(
        block, mesh=mesh, in_specs=(cells,) + (P(),) * 11, out_specs=cells, check_vma=False
    )
```

```python
import functools

import jax
import jax.numpy as jnp
from jax import lax
from jax.experimental import pallas as pl
from jax.experimental.pallas import tpu as pltpu
from jax.sharding import PartitionSpec as P

F32, BF16 = jnp.float32, jnp.bfloat16
FACES, ROWS, COLS, CH, HID = 12, 8, 16, 256, 1024
LANES = 128
TILES, CHANS = 16, 8
STRIDE = 32
FIRST = 8
PADROWS = ROWS + 6
SIDES = 4
STRIP = FACES * 8
RELAYS = (
    (25, 106, 9, 102, 36, 58, 105, 92, 90, 84, 50, 28, 14, 113, 118, 101),
    (70, 22, 114, 62, 100, 66, 12, 65, 34, 10, 20, 38, 30, 17, 97, 57),
)


def pick(values, index):
    if len(values) == 1:
        return values[0]
    low = index % 2 == 0
    return pick([jnp.where(low, a, b) for a, b in zip(values[::2], values[1::2])], index // 2)


def relay_of(block, half):
    device = pick(RELAYS[half], block)
    return {"tile": device // CHANS, "chan": device % CHANS}


def relay_role(i, j):
    device = i * CHANS + j
    place = sum(
        jnp.where(device == relay, 1 + block + 16 * half, 0)
        for half in range(2)
        for block, relay in enumerate(RELAYS[half])
    )
    return place > 0, jnp.maximum(place - 1, 0) % 16, jnp.maximum(place - 1, 0) // 16


def each_quad(body):
    lax.fori_loop(0, FACES // 4, lambda quad, c: (body(quad), c)[1], 0, unroll=3)


def each_pair(body):
    lax.fori_loop(0, FACES // 2, lambda pair, c: (body(pair), c)[1], 0, unroll=3)


def each_face(body):
    lax.fori_loop(0, FACES, lambda face, c: (body(face), c)[1], 0, unroll=3)


def lanes(half):
    return pl.ds(half * LANES, LANES)


def pair_rows(pair):
    return pl.ds(pl.multiple_of(pair * 16, 16), 16)


def kernel(
    fields, neighbour, rotation, conv_weight, conv_bias, norm_gain, norm_shift,
    weight_in, bias_in, weight_out, bias_out, layer_scale,
    out,
    x, nbr, rot, cw, cb, gain, shift, w_in, b_in, w_out, b_out, scale,
    taps, padded, acc, kept, patch, result,
    send_left, send_right, send_edge, send_ends, columns, halo_rows, seam, corner, ends_in,
    relay_in, relay_all, relay_out, relay_first, relay_last,
    local_sems, send_sems, recv_sems, out_sem,
):
    i, j = lax.axis_index("tile"), lax.axis_index("chan")
    has_up, has_down = i > 0, i < TILES - 1
    has_left, has_right = j > 0, j < CHANS - 1
    is_top, is_bottom = i == 0, i == TILES - 1
    is_left, is_right = j == 0, j == CHANS - 1
    is_relay, block, my_half = relay_role(i, j)
    turned_block = 15 - block
    odd = block % 2 == 1

    locals_ = [
        pltpu.make_async_copy(src, dst, local_sems.at[n])
        for n, (src, dst) in enumerate(
            [
                (fields, x), (neighbour, nbr), (rotation, rot), (conv_weight, cw), (conv_bias, cb),
                (norm_gain, gain), (norm_shift, shift), (weight_in, w_in), (bias_in, b_in),
                (weight_out, w_out), (bias_out, b_out), (layer_scale, scale),
            ]
        )
    ]
    locals_[0].start()

    barrier = pltpu.get_barrier_semaphore()

    def greet(tile, chan):
        pl.semaphore_signal(
            barrier, inc=1, device_id={"tile": tile, "chan": chan},
            device_id_type=pl.DeviceIdType.MESH,
        )

    def greet_relays(block_):
        for half in range(2):
            there = relay_of(block_, half)
            greet(there["tile"], there["chan"])

    @pl.when(is_relay)
    def _():
        greet(0, 7 - block // 2)
        greet(block, 0)
        greet(TILES - 1, block // 2)
        greet(turned_block, CHANS - 1)

    def greet_end(to_block):
        greet_relays(to_block(2 * j))
        greet_relays(to_block(2 * j + 1))
        pl.when(has_left)(lambda: greet_relays(to_block(2 * j - 1)))
        pl.when(has_right)(lambda: greet_relays(to_block(2 * j + 2)))

    def greet_side(to_block):
        greet_relays(to_block(i))
        pl.when(has_up)(lambda: greet_relays(to_block(i - 1)))
        pl.when(has_down)(lambda: greet_relays(to_block(i + 1)))

    pl.when(is_top)(lambda: greet_end(lambda t: t))
    pl.when(is_bottom)(lambda: greet_end(lambda t: 15 - t))
    pl.when(is_left)(lambda: greet_side(lambda t: 15 - t))
    pl.when(is_right)(lambda: greet_side(lambda t: t))

    pl.when(has_up)(lambda: greet(i - 1, j))
    pl.when(has_down)(lambda: greet(i + 1, j))
    pl.when(has_left)(lambda: greet(i, j - 1))
    pl.when(has_right)(lambda: greet(i, j + 1))
    for copy in locals_[1:]:
        copy.start()

    def as_int(flag):
        return flag.astype(jnp.int32)

    not_first, not_last = as_int(block > 0), as_int(block < 15)
    expected = (
        as_int(has_up) + as_int(has_down) + as_int(has_left) + as_int(has_right)
        + 4 * as_int(is_top) + 4 * as_int(is_bottom) + 2 * as_int(is_left) + 2 * as_int(is_right)
        + as_int(is_relay)
        * (4 + 2 * (not_first + not_last) + 2 * jnp.where(odd, not_last, not_first))
    )

    locals_[0].wait()

    sublane = lax.broadcasted_iota(jnp.int32, (8, LANES), 0)

    def lower_half(a, b):
        return jnp.where(sublane < 4, a, pltpu.roll(b, 4, 0))

    def upper_half(a, b):
        return jnp.where(sublane < 4, pltpu.roll(a, 4, 0), b)

    def two(a, b):
        return jnp.concatenate([a, b], axis=0).astype(BF16)

    def pack_edge(row_of):
        def body(pair):
            for half in range(2):
                for k in range(3):
                    rows = [x[2 * pair + e, row_of(k), :, lanes(half)].astype(F32) for e in range(2)]
                    for seg in range(2):
                        send_edge[seg, half, k, pair_rows(pair), :] = two(
                            *[row[8 * seg : 8 * seg + 8] for row in rows]
                        )

        each_pair(body)

    pl.when(is_top)(lambda: pack_edge(lambda k: k))
    pl.when(is_bottom)(lambda: pack_edge(lambda k: ROWS - 1 - k))

    def unpack(face):
        for half in range(2):
            for r in range(ROWS):
                padded[face, half, pl.ds((r + 3) * STRIDE + FIRST, COLS), :] = x[
                    face, r, :, lanes(half)
                ].astype(F32)
        zero = jnp.zeros((8, LANES), F32)
        for half in range(2):
            for r in (0, 1, 2, 11, 12, 13):
                padded[face, half, pl.ds(r * STRIDE, 8), :] = zero
                padded[face, half, pl.ds(r * STRIDE + FIRST + COLS, 8), :] = zero

    each_face(unpack)

    @pl.when(is_left | is_right)
    def _():
        def clear(face):
            for half in range(2):
                for r in range(3, 11):
                    for c in (-FIRST, COLS):
                        padded[face, half, pl.ds(r * STRIDE + FIRST + c, 8), :] = jnp.zeros(
                            (8, LANES), F32
                        )

        each_face(clear)

    def column(face, half, first_row, c):
        return padded[face, half, pl.ds(first_row * STRIDE + c + FIRST, 8, stride=STRIDE), :]

    def pack_columns(quad):
        for half in range(2):
            for k in range(3):
                for target, c in ((send_left, k), (send_right, COLS - 1 - k)):
                    cells = [column(4 * quad + e, half, 3, c) for e in range(4)]
                    for e in range(2):
                        target[half, k, pair_rows(2 * quad + e), :] = two(*cells[2 * e : 2 * e + 2])

    each_quad(pack_columns)

    pl.semaphore_wait(barrier, expected)

    def remote(src, dst, send, recv, where):
        return pltpu.make_async_remote_copy(
            src_ref=src, dst_ref=dst, send_sem=send_sems.at[send], recv_sem=recv_sems.at[recv],
            device_id=where, device_id_type=pl.DeviceIdType.MESH,
        )

    COLUMNS, HALO_ROWS, SEAM, CORNER, RELAY, ENDS = 0, 2, 4, 5, 9, 12

    edge_sends = [
        (is_top, [
            remote(send_edge.at[seg, half, k], relay_in.at[k, 0], 6 * k + 2 * seg + half, RELAY + k,
                   relay_of(15 - (2 * j + seg), half))
            for k in range(3) for seg in range(2) for half in range(2)
        ]),
        (is_bottom, [
            remote(send_edge.at[seg, half, k], relay_in.at[k, 2], 6 * k + 2 * seg + half, RELAY + k,
                   relay_of(2 * j + seg, half))
            for k in range(3) for seg in range(2) for half in range(2)
        ]),
        (is_left, [
            remote(send_left.at[half, k], relay_in.at[k, 1], 6 * k + 4 + half, RELAY + k,
                   relay_of(i, half))
            for k in range(3) for half in range(2)
        ]),
        (is_right, [
            remote(send_right.at[half, k], relay_in.at[k, 3], 6 * k + 4 + half, RELAY + k,
                   relay_of(15 - i, half))
            for k in range(3) for half in range(2)
        ]),
    ]
    halo_sends = [
        (has_up, [remote(x.at[:, pl.ds(0, 3)], halo_rows.at[1], 18, HALO_ROWS + 1,
                         {"tile": i - 1, "chan": j})]),
        (has_down, [remote(x.at[:, pl.ds(ROWS - 3, 3)], halo_rows.at[0], 19, HALO_ROWS,
                           {"tile": i + 1, "chan": j})]),
        (has_left, [remote(send_left, columns.at[1], 20, COLUMNS + 1, {"tile": i, "chan": j - 1})]),
        (has_right, [remote(send_right, columns.at[0], 21, COLUMNS, {"tile": i, "chan": j + 1})]),
    ]
    end_sends = [
        (has_left, [remote(send_ends.at[0], ends_in.at[1], 22, ENDS + 1, {"tile": i, "chan": j - 1})]),
        (has_right, [remote(send_ends.at[1], ends_in.at[0], 23, ENDS, {"tile": i, "chan": j + 1})]),
    ]

    def relay_sends(k):
        def pass_on(source, corner_at, n, tile, chan):
            return remote(source, corner.at[corner_at, my_half, k], 24 + 10 * k + n,
                          CORNER + corner_at, {"tile": tile, "chan": chan})

        def to(side, target, n, recv, tile, chan):
            return remote(relay_out.at[k, side], target, 24 + 10 * k + n, recv,
                          {"tile": tile, "chan": chan})

        first, last = relay_first.at[k], relay_last.at[k]
        return [
            (is_relay, [
                to(0, seam.at[block % 2, my_half, k], 0, SEAM, 0, block // 2),
                to(2, seam.at[turned_block % 2, my_half, k], 1, SEAM, TILES - 1, turned_block // 2),
                to(1, columns.at[0, my_half, k], 2, COLUMNS, turned_block, 0),
                to(3, columns.at[1, my_half, k], 3, COLUMNS + 1, block, CHANS - 1),
            ]),
            (is_relay & odd & (block < 15), [
                pass_on(last.at[0], 0, 4, 0, block // 2 + 1),
                pass_on(first.at[2], 3, 5, TILES - 1, turned_block // 2 - 1),
            ]),
            (is_relay & ~odd & (block > 0), [
                pass_on(first.at[0], 2, 4, 0, block // 2 - 1),
                pass_on(last.at[2], 1, 5, TILES - 1, turned_block // 2 + 1),
            ]),
            (is_relay & (turned_block < 15), [pass_on(last.at[1], 0, 6, turned_block + 1, 0)]),
            (is_relay & (turned_block > 0), [pass_on(first.at[1], 1, 7, turned_block - 1, 0)]),
            (is_relay & (block < 15), [pass_on(last.at[3], 2, 8, block + 1, CHANS - 1)]),
            (is_relay & (block > 0), [pass_on(first.at[3], 3, 9, block - 1, CHANS - 1)]),
        ]

    def start_all(sends):
        for condition, copies in sends:
            @pl.when(condition)
            def _():
                for copy in copies:
                    copy.start()

    def arrived(buffer, recv):
        pltpu.make_async_copy(buffer, buffer, recv_sems.at[recv]).wait()

    start_all(edge_sends)
    start_all(halo_sends)

    locals_[3].wait()
    locals_[4].wait()
    for half in range(2):
        for a in range(7):
            for b in range(7):
                taps[half, a * 7 + b] = jnp.broadcast_to(cw[a, pl.ds(b, 1), lanes(half)], (8, LANES))

    def convolve(face, half, group, total, rows, shifts):
        for b in shifts:
            cells = {
                r: padded[face, half, pl.ds(r * STRIDE + FIRST - 3 + b + 8 * group, 8), :]
                for r in rows
            }
            for a in range(7):
                tap = taps[half, a * 7 + b]
                for r in range(ROWS):
                    if r + a in cells and r in total:
                        total[r] = total[r] + tap * cells[r + a]
        return total

    own = range(3, 11)
    near = (range(3, 7), range(4))
    far = (range(3), range(4, 7))

    def add_taps(side, out_rows, rows, shifts, first=False):
        def body(face):
            for half in range(2):
                if first:
                    bias = jnp.broadcast_to(cb[:, lanes(half)], (8, LANES))
                    total = {r: bias for r in out_rows}
                else:
                    total = {r: acc[side, r, face, :, lanes(half)] for r in out_rows}
                for r, value in convolve(face, half, side, total, rows, shifts).items():
                    acc[side, r, face, :, lanes(half)] = value

        each_face(body)

    for side in range(2):
        add_taps(side, range(ROWS), own, near[side], first=True)

    def unpack_rows(end, first_row):
        def body(face):
            for half in range(2):
                for r in range(3):
                    padded[face, half, pl.ds((first_row + r) * STRIDE + FIRST, COLS), :] = halo_rows[
                        end, face, r, :, lanes(half)
                    ].astype(F32)

        each_face(body)

    def unpack_seam(row_of):
        def body(pair):
            for half in range(2):
                for seg in range(2):
                    for k in range(3):
                        both = seam[seg, half, k, pair_rows(pair), :].astype(F32)
                        for e in range(2):
                            padded[
                                2 * pair + e, half, pl.ds(row_of(k) * STRIDE + FIRST + 8 * seg, 8), :
                            ] = both[8 * e : 8 * e + 8]

        each_pair(body)

    def unpack_columns(side):
        def body(pair):
            for half in range(2):
                for k in range(3):
                    both = columns[side, half, k, pair_rows(pair), :].astype(F32)
                    col = -1 - k if side == 0 else COLS + k
                    for e in range(2):
                        padded[
                            2 * pair + e, half,
                            pl.ds(3 * STRIDE + FIRST + col, 8, stride=STRIDE), :
                        ] = both[8 * e : 8 * e + 8]

        each_pair(body)

    def unpack_corner(at, beside, end):
        first_col = -4 if at < 2 else COLS

        def body(quad):
            for half in range(2):
                for k in range(3):
                    cells = corner[at, half, k, pair_rows(quad), :].astype(F32)
                    for e in range(4):
                        if beside:
                            col = -1 - k if at < 2 else COLS + k
                            first, row = (1, 0) if end == 0 else (0, 11)
                            padded[
                                4 * quad + e, half,
                                pl.ds(row * STRIDE + FIRST + col, 3, stride=STRIDE), :
                            ] = cells[4 * e + first : 4 * e + first + 3]
                        else:
                            row = 2 - k if end == 0 else 11 + k
                            padded[
                                4 * quad + e, half, pl.ds(row * STRIDE + FIRST + first_col, 4), :
                            ] = cells[4 * e : 4 * e + 4]

        each_quad(body)

    late = (is_left, is_right)
    any_late = is_left | is_right
    first_end = as_int(is_top)

    def take_rows(end):
        arrived(halo_rows.at[end], HALO_ROWS + end)
        unpack_rows(end, 11 * end)

    def take_seam(end):
        arrived(seam, SEAM)
        unpack_seam((lambda k: 2 - k) if end == 0 else (lambda k: 11 + k))

    def pack_ends(quad):
        for half in range(2):
            for k in range(3):
                for side in range(2):
                    c = k if side == 0 else COLS - 1 - k
                    cells = [
                        jnp.where(
                            sublane < 4,
                            column(4 * quad + e, half, 0, c),
                            column(4 * quad + e, half, 6, c),
                        )
                        for e in range(4)
                    ]
                    for e in range(2):
                        send_ends[side, half, k, pair_rows(2 * quad + e), :] = two(
                            *cells[2 * e : 2 * e + 2]
                        )

    def unpack_ends(side, end):
        def body(pair):
            for half in range(2):
                for k in range(3):
                    cells = ends_in[side, half, k, pair_rows(pair), :].astype(F32)
                    col = -1 - k if side == 0 else COLS + k
                    for e in range(2):
                        first = 8 * e + 5 * end
                        padded[
                            2 * pair + e, half,
                            pl.ds(11 * end * STRIDE + FIRST + col, 3, stride=STRIDE), :
                        ] = cells[first : first + 3]

        each_pair(body)

    def take_columns(side):
        arrived(columns.at[side], COLUMNS + side)
        unpack_columns(side)

    def take_corner(end, side, beside):
        at = 2 * side + end
        arrived(corner.at[at], CORNER + at)
        unpack_corner(at, beside, end)

    def add_end(end, side, shifts):
        if end == 0:
            add_taps(side, range(3), range(3), shifts)
        else:
            add_taps(side, range(5, 8), range(11, 14), shifts)

    for copy in locals_[5:]:
        copy.wait()

    def pointwise(cells):
        shape = cells.shape
        values = cells[...].reshape(-1, CH).astype(BF16).astype(F32)
        mean = jnp.mean(values, axis=-1, keepdims=True)
        apart = values - mean
        spread = jnp.mean(apart * apart, axis=-1, keepdims=True)
        normed = (apart * lax.rsqrt(spread + 1e-6) * gain[...] + shift[...]).astype(BF16)
        hidden = jnp.dot(normed, w_in[...], preferred_element_type=F32) + b_in[...]
        inner_ = hidden * (0.7978845608028654 + 0.035677408136300125 * (hidden * hidden))
        hidden = (hidden * (1.0 + jnp.tanh(inner_))).astype(BF16)
        update = 0.5 * jnp.dot(hidden, w_out[...], preferred_element_type=F32) + b_out[...]
        cells[...] = (scale[...] * update).reshape(shape)

    def finish(first, count):
        def body(face):
            for r in range(count):
                row = first + r
                for half in range(2):
                    update = jnp.concatenate(
                        [acc[side, row, face, :, lanes(half)] for side in range(2)], axis=0
                    )
                    result[face, row, :, lanes(half)] = (
                        x[face, row, :, lanes(half)].astype(F32) + update
                    ).astype(BF16)
            rows = pl.ds(first, count)
            pltpu.make_async_copy(result.at[face, rows], out.at[face, rows], out_sem).start()

        each_face(body)

    def keep(side, rows):
        def body(face):
            for r in rows:
                for half in range(2):
                    kept[half, face, pl.ds(8 * r, 8), :] = acc[side, r, face, :, lanes(half)]

        each_face(body)

    both = pl.ds(0, 2)

    for side in range(2):
        pl.when(~late[side])(functools.partial(take_columns, side))
        add_taps(side, range(ROWS), own, far[side])

    locals_[1].wait()
    locals_[2].wait()

    @pl.when(is_relay)
    def _():
        row = lax.broadcasted_iota(jnp.int32, (STRIP, STRIP), 0)
        col = lax.broadcasted_iota(jnp.int32, (STRIP, STRIP), 1)
        turn = (row // 8 * 8 + 7 - row % 8 == col).astype(BF16)

        def relay(k, carry):
            arrived(relay_in.at[k], RELAY + k)
            for side in range(SIDES):
                strip = relay_in[k, side]
                at = pl.ds(side * FACES, FACES)
                relay_all[0, at] = strip.astype(F32).reshape(FACES, 8, LANES)
                relay_all[1, at] = jnp.dot(turn, strip, preferred_element_type=F32).reshape(
                    FACES, 8, LANES
                )

            def choose(quad):
                for side in range(SIDES):
                    cells = []
                    for e in range(4):
                        source = (side + 6 - rot[side, 4 * quad + e]) & 3
                        same = ((source + 1) & 3) >> 1
                        flip = same if side in (1, 2) else 1 - same
                        cells.append(relay_all[flip, source * FACES + nbr[side, 4 * quad + e]])
                    for e in range(2):
                        relay_out[k, side, pair_rows(2 * quad + e), :] = two(
                            *cells[2 * e : 2 * e + 2]
                        )
                    relay_first[k, side, pair_rows(quad), :] = two(
                        lower_half(*cells[:2]), lower_half(*cells[2:])
                    )
                    relay_last[k, side, pair_rows(quad), :] = two(
                        upper_half(*cells[:2]), upper_half(*cells[2:])
                    )

            each_quad(choose)
            start_all(relay_sends(k))
            return carry

        lax.fori_loop(0, 3, relay, 0)

    for side in range(2):
        pl.when(late[side])(functools.partial(keep, side, range(3, 5)))
    pointwise(acc.at[both, pl.ds(3, 2)])
    pl.when(~any_late)(functools.partial(finish, 3, 2))

    for end in range(2):
        pl.when((has_up, has_down)[end])(functools.partial(take_rows, end))
    each_quad(pack_ends)
    start_all(end_sends)
    for end in range(2):
        @pl.when((has_up, has_down)[end])
        def _():
            for side in range(2):
                add_end(end, side, near[side])

    for side in range(2):
        @pl.when((has_left, has_right)[side])
        def _():
            arrived(ends_in.at[side], ENDS + side)
            for end in range(2):
                pl.when((has_up, has_down)[end])(functools.partial(unpack_ends, side, end))

    def take_end(n, carry):
        end = (first_end + n) % 2
        for an_end in range(2):
            at_end = (is_top, is_bottom)[an_end]

            @pl.when((end == an_end) & ~at_end)
            def _():
                for side in range(2):
                    add_end(an_end, side, far[side])

            @pl.when((end == an_end) & at_end)
            def _():
                take_seam(an_end)
                for side in range(2):
                    pl.when((has_left, has_right)[side])(
                        functools.partial(take_corner, an_end, side, False)
                    )
                    add_end(an_end, side, range(7))

            @pl.when(end == an_end)
            def _():
                for side in range(2):
                    pl.when(late[side])(
                        functools.partial(keep, side, range(3) if an_end == 0 else range(5, 8))
                    )

        pointwise(acc.at[both, pl.ds(5 * end, 3)])
        pl.when(~any_late)(lambda: finish(5 * end, 3))
        return carry

    lax.fori_loop(0, 2, take_end, 0)

    def add_columns(side):
        def body(face):
            for half in range(2):
                cells = [
                    [column(face, half, a, -1 - k if side == 0 else COLS + k) for a in range(7)]
                    for k in range(3)
                ]
                for n in range(3):
                    c = n if side == 0 else 5 + n
                    total = kept[half, face, pl.ds(c, ROWS, stride=8), :]
                    for b in range(3 - n) if side == 0 else range(6 - n, 7):
                        k = 2 - b - n if side == 0 else n + b - 6
                        for a in range(7):
                            total = total + taps[half, a * 7 + b] * cells[k][a]
                    patch[n, face, :, lanes(half)] = total

        each_face(body)

    def put_columns(side):
        def body(face):
            for half in range(2):
                for n in range(3):
                    c = n if side == 0 else 5 + n
                    kept[half, face, pl.ds(c, ROWS, stride=8), :] = patch[n, face, :, lanes(half)]
            near_seam = sublane < 3 if side == 0 else sublane > 4
            for row in range(ROWS):
                for half in range(2):
                    update = [acc[a_side, row, face, :, lanes(half)] for a_side in range(2)]
                    update[side] = jnp.where(
                        near_seam, kept[half, face, pl.ds(8 * row, 8), :], update[side]
                    )
                    result[face, row, :, lanes(half)] = (
                        x[face, row, :, lanes(half)].astype(F32) + jnp.concatenate(update, axis=0)
                    ).astype(BF16)
            pltpu.make_async_copy(result.at[face], out.at[face], out_sem).start()

        each_face(body)

    for side in range(2):
        @pl.when(late[side])
        def _():
            take_columns(side)
            for end in range(2):
                pl.when((has_up, has_down)[end])(functools.partial(take_corner, end, side, True))
            add_columns(side)

    @pl.when(any_late)
    def _():
        pointwise(patch)

    for side in range(2):
        pl.when(late[side])(functools.partial(put_columns, side))

    pltpu.make_async_copy(result, out, out_sem).wait()

    for condition, copies in edge_sends + halo_sends + end_sends:
        @pl.when(condition)
        def _():
            for copy in copies:
                copy.wait_send()

    for k in range(3):
        for condition, copies in relay_sends(k):
            @pl.when(condition)
            def _():
                for copy in copies:
                    copy.wait_send()


def block(fields, neighbour, rotation, conv_weight, conv_bias, norm_gain, norm_shift,
          weight_in, bias_in, weight_out, bias_out, layer_scale):
    def row(vector):
        return vector.reshape(1, -1)

    anywhere = pl.BlockSpec(memory_space=pl.ANY)
    strip = pltpu.VMEM((2, 3, STRIP, LANES), BF16)
    corners = pltpu.VMEM((4, 2, 3, STRIP // 2, LANES), BF16)
    relayed = pltpu.VMEM((3, SIDES, STRIP, LANES), BF16)
    relayed_half = pltpu.VMEM((3, SIDES, STRIP // 2, LANES), BF16)
    return pl.pallas_call(
        kernel,
        out_shape=jax.ShapeDtypeStruct(fields.shape, BF16),
        in_specs=[anywhere] * 12,
        out_specs=anywhere,
        scratch_shapes=[
            pltpu.VMEM(fields.shape, BF16),
            pltpu.SMEM((SIDES, FACES), jnp.int32),
            pltpu.SMEM((SIDES, FACES), jnp.int32),
            pltpu.VMEM((7, 7, CH), F32),
            pltpu.VMEM((1, CH), F32),
            pltpu.VMEM((1, CH), F32),
            pltpu.VMEM((1, CH), F32),
            pltpu.VMEM((CH, HID), BF16),
            pltpu.VMEM((1, HID), F32),
            pltpu.VMEM((HID, CH), BF16),
            pltpu.VMEM((1, CH), F32),
            pltpu.VMEM((1, CH), F32),
            pltpu.VMEM((2, 49, 8, LANES), F32),
            pltpu.VMEM((FACES, 2, PADROWS * STRIDE, LANES), F32),
            pltpu.VMEM((2, ROWS, FACES, 8, CH), F32),
            pltpu.VMEM((2, FACES, 8 * ROWS, LANES), F32),
            pltpu.VMEM((3, FACES, ROWS, CH), F32),
            pltpu.VMEM(fields.shape, BF16),
            strip, strip,
            pltpu.VMEM((2, 2, 3, STRIP, LANES), BF16),
            pltpu.VMEM((2, 2, 3, STRIP, LANES), BF16),
            pltpu.VMEM((2, 2, 3, STRIP, LANES), BF16),
            pltpu.VMEM((2, FACES, 3, COLS, CH), BF16),
            pltpu.VMEM((2, 2, 3, STRIP, LANES), BF16),
            corners,
            pltpu.VMEM((2, 2, 3, STRIP, LANES), BF16),
            relayed,
            pltpu.VMEM((2, SIDES * FACES, 8, LANES), F32),
            relayed, relayed_half, relayed_half,
            pltpu.SemaphoreType.DMA((12,)),
            pltpu.SemaphoreType.DMA((54,)),
            pltpu.SemaphoreType.DMA((14,)),
            pltpu.SemaphoreType.DMA,
        ],
        compiler_params=pltpu.CompilerParams(
            collective_id=0, has_side_effects=True, vmem_limit_bytes=63 * 2**20
        ),
        name="convnext_block",
    )(
        fields, neighbour.T, rotation.T, conv_weight, row(conv_bias), row(norm_gain), row(norm_shift),
        weight_in, row(bias_in), weight_out, row(bias_out), row(layer_scale),
    )


def solution(mesh):
    cells = P(None, "tile", "chan", None)
    return jax.shard_map(
        block, mesh=mesh, in_specs=(cells,) + (P(),) * 11, out_specs=cells, check_vma=False
    )
```

```python
import functools

import jax
import jax.numpy as jnp
from jax import lax
from jax.experimental import pallas as pl
from jax.experimental.pallas import tpu as pltpu
from jax.sharding import PartitionSpec as P

F32, BF16 = jnp.float32, jnp.bfloat16
FACES, ROWS, COLS, CH, HID = 12, 8, 16, 256, 1024
LANES = 128
TILES, CHANS = 16, 8
STRIDE = 32
FIRST = 8
PADROWS = ROWS + 6
SIDES = 4
STRIP = FACES * 8
RELAYS = (
    (25, 106, 9, 102, 36, 58, 105, 92, 90, 84, 50, 28, 14, 113, 118, 101),
    (70, 22, 114, 62, 100, 66, 12, 65, 34, 10, 20, 38, 30, 17, 97, 57),
)


def pick(values, index):
    if len(values) == 1:
        return values[0]
    low = index % 2 == 0
    return pick([jnp.where(low, a, b) for a, b in zip(values[::2], values[1::2])], index // 2)


def relay_of(block, half):
    device = pick(RELAYS[half], block)
    return {"tile": device // CHANS, "chan": device % CHANS}


def relay_role(i, j):
    device = i * CHANS + j
    place = sum(
        jnp.where(device == relay, 1 + block + 16 * half, 0)
        for half in range(2)
        for block, relay in enumerate(RELAYS[half])
    )
    return place > 0, jnp.maximum(place - 1, 0) % 16, jnp.maximum(place - 1, 0) // 16


def each_quad(body):
    lax.fori_loop(0, FACES // 4, lambda quad, c: (body(quad), c)[1], 0, unroll=3)


def each_pair(body):
    lax.fori_loop(0, FACES // 2, lambda pair, c: (body(pair), c)[1], 0, unroll=3)


def each_face(body):
    lax.fori_loop(0, FACES, lambda face, c: (body(face), c)[1], 0, unroll=3)


def lanes(half):
    return pl.ds(half * LANES, LANES)


def pair_rows(pair):
    return pl.ds(pl.multiple_of(pair * 16, 16), 16)


def kernel(
    fields, neighbour, rotation, conv_weight, conv_bias, norm_gain, norm_shift,
    weight_in, bias_in, weight_out, bias_out, layer_scale,
    out,
    x, nbr, rot, cw, cb, gain, shift, w_in, b_in, w_out, b_out, scale,
    taps, padded, acc, kept, patch, result,
    send_left, send_right, send_edge, send_ends, columns, halo_rows, seam, corner, ends_in,
    relay_in, relay_all, relay_out, relay_first, relay_last,
    local_sems, send_sems, recv_sems, out_sem,
):
    i, j = lax.axis_index("tile"), lax.axis_index("chan")
    has_up, has_down = i > 0, i < TILES - 1
    has_left, has_right = j > 0, j < CHANS - 1
    is_top, is_bottom = i == 0, i == TILES - 1
    is_left, is_right = j == 0, j == CHANS - 1
    is_relay, block, my_half = relay_role(i, j)
    turned_block = 15 - block
    odd = block % 2 == 1

    locals_ = [
        pltpu.make_async_copy(src, dst, local_sems.at[n])
        for n, (src, dst) in enumerate(
            [
                (fields, x), (neighbour, nbr), (rotation, rot), (conv_weight, cw), (conv_bias, cb),
                (norm_gain, gain), (norm_shift, shift), (weight_in, w_in), (bias_in, b_in),
                (weight_out, w_out), (bias_out, b_out), (layer_scale, scale),
            ]
        )
    ]
    locals_[0].start()

    barrier = pltpu.get_barrier_semaphore()

    def greet(tile, chan):
        pl.semaphore_signal(
            barrier, inc=1, device_id={"tile": tile, "chan": chan},
            device_id_type=pl.DeviceIdType.MESH,
        )

    def greet_relays(block_):
        for half in range(2):
            there = relay_of(block_, half)
            greet(there["tile"], there["chan"])

    @pl.when(is_relay)
    def _():
        greet(0, 7 - block // 2)
        greet(block, 0)
        greet(TILES - 1, block // 2)
        greet(turned_block, CHANS - 1)

    def greet_end(to_block):
        greet_relays(to_block(2 * j))
        greet_relays(to_block(2 * j + 1))
        pl.when(has_left)(lambda: greet_relays(to_block(2 * j - 1)))
        pl.when(has_right)(lambda: greet_relays(to_block(2 * j + 2)))

    def greet_side(to_block):
        greet_relays(to_block(i))
        pl.when(has_up)(lambda: greet_relays(to_block(i - 1)))
        pl.when(has_down)(lambda: greet_relays(to_block(i + 1)))

    pl.when(is_top)(lambda: greet_end(lambda t: t))
    pl.when(is_bottom)(lambda: greet_end(lambda t: 15 - t))
    pl.when(is_left)(lambda: greet_side(lambda t: 15 - t))
    pl.when(is_right)(lambda: greet_side(lambda t: t))

    pl.when(has_up)(lambda: greet(i - 1, j))
    pl.when(has_down)(lambda: greet(i + 1, j))
    pl.when(has_left)(lambda: greet(i, j - 1))
    pl.when(has_right)(lambda: greet(i, j + 1))
    for copy in locals_[1:]:
        copy.start()

    def as_int(flag):
        return flag.astype(jnp.int32)

    not_first, not_last = as_int(block > 0), as_int(block < 15)
    expected = (
        as_int(has_up) + as_int(has_down) + as_int(has_left) + as_int(has_right)
        + 4 * as_int(is_top) + 4 * as_int(is_bottom) + 2 * as_int(is_left) + 2 * as_int(is_right)
        + as_int(is_relay)
        * (4 + 2 * (not_first + not_last) + 2 * jnp.where(odd, not_last, not_first))
    )

    locals_[0].wait()

    sublane = lax.broadcasted_iota(jnp.int32, (8, LANES), 0)

    def lower_half(a, b):
        return jnp.where(sublane < 4, a, pltpu.roll(b, 4, 0))

    def upper_half(a, b):
        return jnp.where(sublane < 4, pltpu.roll(a, 4, 0), b)

    def two(a, b):
        return jnp.concatenate([a, b], axis=0).astype(BF16)

    def pack_edge(row_of):
        def body(pair):
            for half in range(2):
                for k in range(3):
                    rows = [x[2 * pair + e, row_of(k), :, lanes(half)].astype(F32) for e in range(2)]
                    for seg in range(2):
                        send_edge[seg, half, k, pair_rows(pair), :] = two(
                            *[row[8 * seg : 8 * seg + 8] for row in rows]
                        )

        each_pair(body)

    pl.when(is_top)(lambda: pack_edge(lambda k: k))
    pl.when(is_bottom)(lambda: pack_edge(lambda k: ROWS - 1 - k))

    def unpack(face):
        for half in range(2):
            for r in range(ROWS):
                padded[face, half, pl.ds((r + 3) * STRIDE + FIRST, COLS), :] = x[
                    face, r, :, lanes(half)
                ].astype(F32)
        zero = jnp.zeros((8, LANES), F32)
        for half in range(2):
            for r in (0, 1, 2, 11, 12, 13):
                padded[face, half, pl.ds(r * STRIDE, 8), :] = zero
                padded[face, half, pl.ds(r * STRIDE + FIRST + COLS, 8), :] = zero

    each_face(unpack)

    @pl.when(is_left | is_right)
    def _():
        def clear(face):
            for half in range(2):
                for r in range(3, 11):
                    for c in (-FIRST, COLS):
                        padded[face, half, pl.ds(r * STRIDE + FIRST + c, 8), :] = jnp.zeros(
                            (8, LANES), F32
                        )

        each_face(clear)

    def column(face, half, first_row, c):
        return padded[face, half, pl.ds(first_row * STRIDE + c + FIRST, 8, stride=STRIDE), :]

    def pack_columns(quad):
        for half in range(2):
            for k in range(3):
                for target, c in ((send_left, k), (send_right, COLS - 1 - k)):
                    cells = [column(4 * quad + e, half, 3, c) for e in range(4)]
                    for e in range(2):
                        target[half, k, pair_rows(2 * quad + e), :] = two(*cells[2 * e : 2 * e + 2])

    each_quad(pack_columns)

    pl.semaphore_wait(barrier, expected)

    def remote(src, dst, send, recv, where):
        return pltpu.make_async_remote_copy(
            src_ref=src, dst_ref=dst, send_sem=send_sems.at[send], recv_sem=recv_sems.at[recv],
            device_id=where, device_id_type=pl.DeviceIdType.MESH,
        )

    COLUMNS, HALO_ROWS, SEAM, CORNER, RELAY, ENDS = 0, 2, 4, 5, 9, 12

    edge_sends = [
        (is_top, [
            remote(send_edge.at[seg, half, k], relay_in.at[k, 0], 6 * k + 2 * seg + half, RELAY + k,
                   relay_of(15 - (2 * j + seg), half))
            for k in range(3) for seg in range(2) for half in range(2)
        ]),
        (is_bottom, [
            remote(send_edge.at[seg, half, k], relay_in.at[k, 2], 6 * k + 2 * seg + half, RELAY + k,
                   relay_of(2 * j + seg, half))
            for k in range(3) for seg in range(2) for half in range(2)
        ]),
        (is_left, [
            remote(send_left.at[half, k], relay_in.at[k, 1], 6 * k + 4 + half, RELAY + k,
                   relay_of(i, half))
            for k in range(3) for half in range(2)
        ]),
        (is_right, [
            remote(send_right.at[half, k], relay_in.at[k, 3], 6 * k + 4 + half, RELAY + k,
                   relay_of(15 - i, half))
            for k in range(3) for half in range(2)
        ]),
    ]
    halo_sends = [
        (has_up, [remote(x.at[:, pl.ds(0, 3)], halo_rows.at[1], 18, HALO_ROWS + 1,
                         {"tile": i - 1, "chan": j})]),
        (has_down, [remote(x.at[:, pl.ds(ROWS - 3, 3)], halo_rows.at[0], 19, HALO_ROWS,
                           {"tile": i + 1, "chan": j})]),
        (has_left, [remote(send_left, columns.at[1], 20, COLUMNS + 1, {"tile": i, "chan": j - 1})]),
        (has_right, [remote(send_right, columns.at[0], 21, COLUMNS, {"tile": i, "chan": j + 1})]),
    ]
    end_sends = [
        (has_left, [remote(send_ends.at[0], ends_in.at[1], 22, ENDS + 1, {"tile": i, "chan": j - 1})]),
        (has_right, [remote(send_ends.at[1], ends_in.at[0], 23, ENDS, {"tile": i, "chan": j + 1})]),
    ]

    def relay_sends(k):
        def pass_on(source, corner_at, n, tile, chan):
            return remote(source, corner.at[corner_at, my_half, k], 24 + 10 * k + n,
                          CORNER + corner_at, {"tile": tile, "chan": chan})

        def to(side, target, n, recv, tile, chan):
            return remote(relay_out.at[k, side], target, 24 + 10 * k + n, recv,
                          {"tile": tile, "chan": chan})

        first, last = relay_first.at[k], relay_last.at[k]
        return [
            (is_relay, [
                to(0, seam.at[block % 2, my_half, k], 0, SEAM, 0, block // 2),
                to(2, seam.at[turned_block % 2, my_half, k], 1, SEAM, TILES - 1, turned_block // 2),
                to(1, columns.at[0, my_half, k], 2, COLUMNS, turned_block, 0),
                to(3, columns.at[1, my_half, k], 3, COLUMNS + 1, block, CHANS - 1),
            ]),
            (is_relay & odd & (block < 15), [
                pass_on(last.at[0], 0, 4, 0, block // 2 + 1),
                pass_on(first.at[2], 3, 5, TILES - 1, turned_block // 2 - 1),
            ]),
            (is_relay & ~odd & (block > 0), [
                pass_on(first.at[0], 2, 4, 0, block // 2 - 1),
                pass_on(last.at[2], 1, 5, TILES - 1, turned_block // 2 + 1),
            ]),
            (is_relay & (turned_block < 15), [pass_on(last.at[1], 0, 6, turned_block + 1, 0)]),
            (is_relay & (turned_block > 0), [pass_on(first.at[1], 1, 7, turned_block - 1, 0)]),
            (is_relay & (block < 15), [pass_on(last.at[3], 2, 8, block + 1, CHANS - 1)]),
            (is_relay & (block > 0), [pass_on(first.at[3], 3, 9, block - 1, CHANS - 1)]),
        ]

    def start_all(sends):
        for condition, copies in sends:
            @pl.when(condition)
            def _():
                for copy in copies:
                    copy.start()

    def arrived(buffer, recv):
        pltpu.make_async_copy(buffer, buffer, recv_sems.at[recv]).wait()

    start_all(edge_sends)
    start_all(halo_sends[2:])
    start_all(halo_sends[:2])

    locals_[3].wait()
    locals_[4].wait()
    for half in range(2):
        for a in range(7):
            for b in range(7):
                taps[half, a * 7 + b] = jnp.broadcast_to(cw[a, pl.ds(b, 1), lanes(half)], (8, LANES))

    def convolve(face, half, group, total, rows, shifts):
        for b in shifts:
            cells = {
                r: padded[face, half, pl.ds(r * STRIDE + FIRST - 3 + b + 8 * group, 8), :]
                for r in rows
            }
            for a in range(7):
                tap = taps[half, a * 7 + b]
                for r in range(ROWS):
                    if r + a in cells and r in total:
                        total[r] = total[r] + tap * cells[r + a]
        return total

    own = range(3, 11)
    near = (range(3, 7), range(4))
    far = (range(3), range(4, 7))

    def add_taps(side, out_rows, rows, shifts, first=False):
        def body(face):
            for half in range(2):
                if first:
                    bias = jnp.broadcast_to(cb[:, lanes(half)], (8, LANES))
                    total = {r: bias for r in out_rows}
                else:
                    total = {r: acc[side, r, face, :, lanes(half)] for r in out_rows}
                for r, value in convolve(face, half, side, total, rows, shifts).items():
                    acc[side, r, face, :, lanes(half)] = value

        each_face(body)

    for side in range(2):
        add_taps(side, range(ROWS), own, near[side], first=True)

    def unpack_rows(end, first_row):
        def body(face):
            for half in range(2):
                for r in range(3):
                    padded[face, half, pl.ds((first_row + r) * STRIDE + FIRST, COLS), :] = halo_rows[
                        end, face, r, :, lanes(half)
                    ].astype(F32)

        each_face(body)

    def unpack_seam(row_of):
        def body(pair):
            for half in range(2):
                for seg in range(2):
                    for k in range(3):
                        both = seam[seg, half, k, pair_rows(pair), :].astype(F32)
                        for e in range(2):
                            padded[
                                2 * pair + e, half, pl.ds(row_of(k) * STRIDE + FIRST + 8 * seg, 8), :
                            ] = both[8 * e : 8 * e + 8]

        each_pair(body)

    def unpack_columns(side):
        def body(pair):
            for half in range(2):
                for k in range(3):
                    both = columns[side, half, k, pair_rows(pair), :].astype(F32)
                    col = -1 - k if side == 0 else COLS + k
                    for e in range(2):
                        padded[
                            2 * pair + e, half,
                            pl.ds(3 * STRIDE + FIRST + col, 8, stride=STRIDE), :
                        ] = both[8 * e : 8 * e + 8]

        each_pair(body)

    def unpack_corner(at, beside, end):
        first_col = -4 if at < 2 else COLS

        def body(quad):
            for half in range(2):
                for k in range(3):
                    cells = corner[at, half, k, pair_rows(quad), :].astype(F32)
                    for e in range(4):
                        if beside:
                            col = -1 - k if at < 2 else COLS + k
                            first, row = (1, 0) if end == 0 else (0, 11)
                            padded[
                                4 * quad + e, half,
                                pl.ds(row * STRIDE + FIRST + col, 3, stride=STRIDE), :
                            ] = cells[4 * e + first : 4 * e + first + 3]
                        else:
                            row = 2 - k if end == 0 else 11 + k
                            padded[
                                4 * quad + e, half, pl.ds(row * STRIDE + FIRST + first_col, 4), :
                            ] = cells[4 * e : 4 * e + 4]

        each_quad(body)

    late = (is_left, is_right)
    any_late = is_left | is_right
    first_end = as_int(is_top)

    def take_rows(end):
        arrived(halo_rows.at[end], HALO_ROWS + end)
        unpack_rows(end, 11 * end)

    def take_seam(end):
        arrived(seam, SEAM)
        unpack_seam((lambda k: 2 - k) if end == 0 else (lambda k: 11 + k))

    def pack_ends(quad):
        for half in range(2):
            for k in range(3):
                for side in range(2):
                    c = k if side == 0 else COLS - 1 - k
                    cells = [
                        jnp.where(
                            sublane < 4,
                            column(4 * quad + e, half, 0, c),
                            column(4 * quad + e, half, 6, c),
                        )
                        for e in range(4)
                    ]
                    for e in range(2):
                        send_ends[side, half, k, pair_rows(2 * quad + e), :] = two(
                            *cells[2 * e : 2 * e + 2]
                        )

    def unpack_ends(side, end):
        def body(pair):
            for half in range(2):
                for k in range(3):
                    cells = ends_in[side, half, k, pair_rows(pair), :].astype(F32)
                    col = -1 - k if side == 0 else COLS + k
                    for e in range(2):
                        first = 8 * e + 5 * end
                        padded[
                            2 * pair + e, half,
                            pl.ds(11 * end * STRIDE + FIRST + col, 3, stride=STRIDE), :
                        ] = cells[first : first + 3]

        each_pair(body)

    def take_columns(side):
        arrived(columns.at[side], COLUMNS + side)
        unpack_columns(side)

    def take_corner(end, side, beside):
        at = 2 * side + end
        arrived(corner.at[at], CORNER + at)
        unpack_corner(at, beside, end)

    def add_end(end, side, shifts):
        if end == 0:
            add_taps(side, range(3), range(3), shifts)
        else:
            add_taps(side, range(5, 8), range(11, 14), shifts)

    for copy in locals_[5:]:
        copy.wait()

    def pointwise(cells):
        shape = cells.shape
        values = cells[...].reshape(-1, CH).astype(BF16).astype(F32)
        mean = jnp.mean(values, axis=-1, keepdims=True)
        apart = values - mean
        spread = jnp.mean(apart * apart, axis=-1, keepdims=True)
        normed = (apart * lax.rsqrt(spread + 1e-6) * gain[...] + shift[...]).astype(BF16)
        hidden = jnp.dot(normed, w_in[...], preferred_element_type=F32) + b_in[...]
        inner_ = hidden * (0.7978845608028654 + 0.035677408136300125 * (hidden * hidden))
        hidden = (hidden * (1.0 + jnp.tanh(inner_))).astype(BF16)
        update = 0.5 * jnp.dot(hidden, w_out[...], preferred_element_type=F32) + b_out[...]
        cells[...] = (scale[...] * update).reshape(shape)

    def finish(first, count):
        def body(face):
            for r in range(count):
                row = first + r
                for half in range(2):
                    update = jnp.concatenate(
                        [acc[side, row, face, :, lanes(half)] for side in range(2)], axis=0
                    )
                    result[face, row, :, lanes(half)] = (
                        x[face, row, :, lanes(half)].astype(F32) + update
                    ).astype(BF16)
            rows = pl.ds(first, count)
            pltpu.make_async_copy(result.at[face, rows], out.at[face, rows], out_sem).start()

        each_face(body)

    def keep(side, rows):
        def body(face):
            for r in rows:
                for half in range(2):
                    kept[half, face, pl.ds(8 * r, 8), :] = acc[side, r, face, :, lanes(half)]

        each_face(body)

    both = pl.ds(0, 2)

    for side in range(2):
        pl.when(~late[side])(functools.partial(take_columns, side))
        add_taps(side, range(ROWS), own, far[side])

    locals_[1].wait()
    locals_[2].wait()

    @pl.when(is_relay)
    def _():
        row = lax.broadcasted_iota(jnp.int32, (STRIP, STRIP), 0)
        col = lax.broadcasted_iota(jnp.int32, (STRIP, STRIP), 1)
        turn = (row // 8 * 8 + 7 - row % 8 == col).astype(BF16)

        def relay(k, carry):
            arrived(relay_in.at[k], RELAY + k)
            for side in range(SIDES):
                strip = relay_in[k, side]
                at = pl.ds(side * FACES, FACES)
                relay_all[0, at] = strip.astype(F32).reshape(FACES, 8, LANES)
                relay_all[1, at] = jnp.dot(turn, strip, preferred_element_type=F32).reshape(
                    FACES, 8, LANES
                )

            def choose(quad):
                for side in range(SIDES):
                    cells = []
                    for e in range(4):
                        source = (side + 6 - rot[side, 4 * quad + e]) & 3
                        same = ((source + 1) & 3) >> 1
                        flip = same if side in (1, 2) else 1 - same
                        cells.append(relay_all[flip, source * FACES + nbr[side, 4 * quad + e]])
                    for e in range(2):
                        relay_out[k, side, pair_rows(2 * quad + e), :] = two(
                            *cells[2 * e : 2 * e + 2]
                        )
                    relay_first[k, side, pair_rows(quad), :] = two(
                        lower_half(*cells[:2]), lower_half(*cells[2:])
                    )
                    relay_last[k, side, pair_rows(quad), :] = two(
                        upper_half(*cells[:2]), upper_half(*cells[2:])
                    )

            each_quad(choose)
            start_all(relay_sends(k))
            return carry

        lax.fori_loop(0, 3, relay, 0)

    for side in range(2):
        pl.when(late[side])(functools.partial(keep, side, range(3, 5)))
    pointwise(acc.at[both, pl.ds(3, 2)])
    pl.when(~any_late)(functools.partial(finish, 3, 2))

    for end in range(2):
        pl.when((has_up, has_down)[end])(functools.partial(take_rows, end))
    each_quad(pack_ends)
    start_all(end_sends)
    for end in range(2):
        @pl.when((has_up, has_down)[end])
        def _():
            for side in range(2):
                add_end(end, side, near[side])

    for side in range(2):
        @pl.when((has_left, has_right)[side])
        def _():
            arrived(ends_in.at[side], ENDS + side)
            for end in range(2):
                pl.when((has_up, has_down)[end])(functools.partial(unpack_ends, side, end))

    def take_end(n, carry):
        end = (first_end + n) % 2
        for an_end in range(2):
            at_end = (is_top, is_bottom)[an_end]

            @pl.when((end == an_end) & ~at_end)
            def _():
                for side in range(2):
                    add_end(an_end, side, far[side])

            @pl.when((end == an_end) & at_end)
            def _():
                take_seam(an_end)
                for side in range(2):
                    add_end(an_end, side, near[side])
                for side in range(2):
                    pl.when((has_left, has_right)[side])(
                        functools.partial(take_corner, an_end, side, False)
                    )
                    add_end(an_end, side, far[side])

            @pl.when(end == an_end)
            def _():
                for side in range(2):
                    pl.when(late[side])(
                        functools.partial(keep, side, range(3) if an_end == 0 else range(5, 8))
                    )

        pointwise(acc.at[both, pl.ds(5 * end, 3)])
        pl.when(~any_late)(lambda: finish(5 * end, 3))
        return carry

    lax.fori_loop(0, 2, take_end, 0)

    def add_columns(side):
        def body(face):
            for half in range(2):
                cells = [
                    [column(face, half, a, -1 - k if side == 0 else COLS + k) for a in range(7)]
                    for k in range(3)
                ]
                for n in range(3):
                    c = n if side == 0 else 5 + n
                    total = kept[half, face, pl.ds(c, ROWS, stride=8), :]
                    for b in range(3 - n) if side == 0 else range(6 - n, 7):
                        k = 2 - b - n if side == 0 else n + b - 6
                        for a in range(7):
                            total = total + taps[half, a * 7 + b] * cells[k][a]
                    patch[n, face, :, lanes(half)] = total

        each_face(body)

    def put_columns(side):
        def body(face):
            for half in range(2):
                for n in range(3):
                    c = n if side == 0 else 5 + n
                    kept[half, face, pl.ds(c, ROWS, stride=8), :] = patch[n, face, :, lanes(half)]
            near_seam = sublane < 3 if side == 0 else sublane > 4
            for row in range(ROWS):
                for half in range(2):
                    update = [acc[a_side, row, face, :, lanes(half)] for a_side in range(2)]
                    update[side] = jnp.where(
                        near_seam, kept[half, face, pl.ds(8 * row, 8), :], update[side]
                    )
                    result[face, row, :, lanes(half)] = (
                        x[face, row, :, lanes(half)].astype(F32) + jnp.concatenate(update, axis=0)
                    ).astype(BF16)
            pltpu.make_async_copy(result.at[face], out.at[face], out_sem).start()

        each_face(body)

    for side in range(2):
        @pl.when(late[side])
        def _():
            take_columns(side)
            for end in range(2):
                pl.when((has_up, has_down)[end])(functools.partial(take_corner, end, side, True))
            add_columns(side)

    @pl.when(any_late)
    def _():
        pointwise(patch)

    for side in range(2):
        pl.when(late[side])(functools.partial(put_columns, side))

    pltpu.make_async_copy(result, out, out_sem).wait()

    for condition, copies in edge_sends + halo_sends + end_sends:
        @pl.when(condition)
        def _():
            for copy in copies:
                copy.wait_send()

    for k in range(3):
        for condition, copies in relay_sends(k):
            @pl.when(condition)
            def _():
                for copy in copies:
                    copy.wait_send()


def block(fields, neighbour, rotation, conv_weight, conv_bias, norm_gain, norm_shift,
          weight_in, bias_in, weight_out, bias_out, layer_scale):
    def row(vector):
        return vector.reshape(1, -1)

    anywhere = pl.BlockSpec(memory_space=pl.ANY)
    strip = pltpu.VMEM((2, 3, STRIP, LANES), BF16)
    corners = pltpu.VMEM((4, 2, 3, STRIP // 2, LANES), BF16)
    relayed = pltpu.VMEM((3, SIDES, STRIP, LANES), BF16)
    relayed_half = pltpu.VMEM((3, SIDES, STRIP // 2, LANES), BF16)
    return pl.pallas_call(
        kernel,
        out_shape=jax.ShapeDtypeStruct(fields.shape, BF16),
        in_specs=[anywhere] * 12,
        out_specs=anywhere,
        scratch_shapes=[
            pltpu.VMEM(fields.shape, BF16),
            pltpu.SMEM((SIDES, FACES), jnp.int32),
            pltpu.SMEM((SIDES, FACES), jnp.int32),
            pltpu.VMEM((7, 7, CH), F32),
            pltpu.VMEM((1, CH), F32),
            pltpu.VMEM((1, CH), F32),
            pltpu.VMEM((1, CH), F32),
            pltpu.VMEM((CH, HID), BF16),
            pltpu.VMEM((1, HID), F32),
            pltpu.VMEM((HID, CH), BF16),
            pltpu.VMEM((1, CH), F32),
            pltpu.VMEM((1, CH), F32),
            pltpu.VMEM((2, 49, 8, LANES), F32),
            pltpu.VMEM((FACES, 2, (PADROWS + 2) * STRIDE, LANES), F32),
            pltpu.VMEM((2, ROWS, FACES, 8, CH), F32),
            pltpu.VMEM((2, FACES, 8 * ROWS + 8, LANES), F32),
            pltpu.VMEM((3, FACES, ROWS, CH), F32),
            pltpu.VMEM(fields.shape, BF16),
            strip, strip,
            pltpu.VMEM((2, 2, 3, STRIP, LANES), BF16),
            pltpu.VMEM((2, 2, 3, STRIP, LANES), BF16),
            pltpu.VMEM((2, 2, 3, STRIP, LANES), BF16),
            pltpu.VMEM((2, FACES, 3, COLS, CH), BF16),
            pltpu.VMEM((2, 2, 3, STRIP, LANES), BF16),
            corners,
            pltpu.VMEM((2, 2, 3, STRIP, LANES), BF16),
            relayed,
            pltpu.VMEM((2, SIDES * FACES, 8, LANES), F32),
            relayed, relayed_half, relayed_half,
            pltpu.SemaphoreType.DMA((12,)),
            pltpu.SemaphoreType.DMA((54,)),
            pltpu.SemaphoreType.DMA((14,)),
            pltpu.SemaphoreType.DMA,
        ],
        compiler_params=pltpu.CompilerParams(
            collective_id=0, has_side_effects=True, vmem_limit_bytes=63 * 2**20
        ),
        name="convnext_block",
    )(
        fields, neighbour.T, rotation.T, conv_weight, row(conv_bias), row(norm_gain), row(norm_shift),
        weight_in, row(bias_in), weight_out, row(bias_out), row(layer_scale),
    )


def solution(mesh):
    cells = P(None, "tile", "chan", None)
    return jax.shard_map(
        block, mesh=mesh, in_specs=(cells,) + (P(),) * 11, out_specs=cells, check_vma=False
    )
```
